256 devices in a mesh: ctx: 32 (over y_hi, z, core), tp: 8 (over x, y_lo).
Axes of the slice: x: 4, y: 4 (y_hi: 2, y_lo: 2; y = y_hi * 2 + y_lo), z: 8, core: 2. Of those that a mesh axis runs over, the one named last changes fastest.
Arguments:
- queries: bfloat16 [512, 16384], P('ctx', 'tp'), may hold values from -32 to 32
- rotated_new_keys: bfloat16 [512, 1024], P('ctx', 'tp'), may hold values from -32 to 32
- fresh_token_values: bfloat16 [512, 1024], P('ctx', 'tp'), may hold values from -6 to 6
- paged_key_cache: bfloat16 [384, 128, 1024], P('ctx', None, 'tp'), may hold values from -6 to 6
- paged_value_cache: bfloat16 [384, 128, 1024], P('ctx', None, 'tp'), may hold values from -6 to 6
- out_weight: bfloat16 [16384, 16384], P('tp', 'ctx'), may hold values from -0.375 to 0.375
- prefix_len: int32 [2], replicated, may hold values from 6144 to 24576, as said below
- new_count: int32 [2], replicated, may hold values from 64 to 256, as said below
- page_map: int32 [384], replicated, may hold values from 0 to 383, each once
Outputs:
- projected: bfloat16 [512, 16384], P('tp', 'ctx')
The draws below stay inside these ranges and needn't reach their ends.
Inputs may be any that keep to these rules, and one draw needn't show every extreme that they name: `prefix_len`: one request's cached prefix is exactly 24576. `new_count`: one request has exactly 256 new tokens. `page_map`: a permutation of the logical pages.
All inputs are finite; a program needn't handle non-finite values.
Results may differ from the reference program's by a relative error of at most 0.019.
Values may be sent and summed in bfloat16 or wider, within the bound.
No kernel may reach another device: no remote copies, remote signals or barrier semaphores. Data moves between devices by JAX's collectives and lax.ppermute only.
A program may use at most 128 MiB of HBM per device.

```python
import jax
import jax.numpy as jnp
from jax import lax

D = 16384
QUERY_HEADS = 128
KEY_VALUE_HEADS = 8
HEAD_WIDTH = 128
QUERY_GROUP = 16
REQS = 2
PAGE_SLOTS = 128
TOKENS_PER_INDEX = 16
PAGES_PER_INDEX = 12
NEW_TOKENS = 512
NEW = 256
TOTAL_PAGES = 384
CACHE_REQ = 24576
N_CTX = 32


def draw_queries(key, part):
    key = jax.random.fold_in(key, 1)
    final_output = jnp.clip(2.0 * jax.random.normal(key, (NEW_TOKENS, QUERY_HEADS * HEAD_WIDTH), jnp.float32), -12.0, 12.0)
    return final_output.astype(jnp.bfloat16)


def draw_rotated_new_keys(key, part):
    key = jax.random.fold_in(key, 2)
    final_output = jnp.clip(jax.random.normal(key, (NEW_TOKENS, KEY_VALUE_HEADS * HEAD_WIDTH), jnp.float32), -6.0, 6.0)
    return final_output.astype(jnp.bfloat16)


def draw_prefix_len(key, part):
    key = jax.random.fold_in(key, 3)
    first_operand, second_operand = jax.random.split(key)
    longest = jax.random.randint(first_operand, (), 0, REQS)
    others = jax.random.randint(second_operand, (REQS,), CACHE_REQ // 4, CACHE_REQ + 1)
    return jnp.where(jnp.arange(REQS) == longest, CACHE_REQ, others).astype(jnp.int32)


def draw_new_count(key, part):
    key = jax.random.fold_in(key, 4)
    first_operand, second_operand = jax.random.split(key)
    longest = jax.random.randint(first_operand, (), 0, REQS)
    others = jax.random.randint(second_operand, (REQS,), NEW // 4, NEW + 1)
    return jnp.where(jnp.arange(REQS) == longest, NEW, others).astype(jnp.int32)


def levels(rng, shape, cuts, low, top_value):
    loudness = 1.0
    for dim, shards_of in cuts:
        steps = jax.random.uniform(jax.random.fold_in(jax.random.fold_in(rng, 6), dim), (shards_of,), jnp.float32, low / len(cuts), top_value / len(cuts))
        loudness = loudness * jnp.repeat(jnp.exp(steps), shape[dim] // shards_of).reshape((-1,) + (1,) * (len(shape) - 1 - dim))
    return loudness


def normal_values(key, dims, scale, most, pieces=(), kind=jnp.bfloat16):
    factor_of = levels(key, dims, pieces, -0.22, 0.18) if pieces else 1.0
    entries = jax.random.normal(key, dims, jnp.float32) * scale * factor_of
    return jnp.minimum(jnp.maximum(entries, -most), most).astype(kind)


def setup_inputs(seed: int = 0) -> dict:
    key_of = jax.random.split(jax.random.key(seed), 10)
    return {
        "queries": draw_queries(jax.random.fold_in(key_of[9], 71), 0),
        "rotated_new_keys": draw_rotated_new_keys(jax.random.fold_in(key_of[9], 71), 0),
        "fresh_token_values": normal_values(key_of[2], (NEW_TOKENS, KEY_VALUE_HEADS * HEAD_WIDTH), 1.0, 6.0, ((0, 32), (1, 8))),
        "paged_key_cache": normal_values(key_of[3], (TOTAL_PAGES, PAGE_SLOTS, KEY_VALUE_HEADS * HEAD_WIDTH), 1.0, 6.0, ((0, 32), (2, 8))),
        "paged_value_cache": normal_values(key_of[4], (TOTAL_PAGES, PAGE_SLOTS, KEY_VALUE_HEADS * HEAD_WIDTH), 1.0, 6.0, ((0, 32), (2, 8))),
        "out_weight": normal_values(key_of[5], (QUERY_HEADS * HEAD_WIDTH, D), (2 * HEAD_WIDTH) ** -0.5, 0.375, ((0, 8), (1, 32))),
        "prefix_len": draw_prefix_len(jax.random.fold_in(key_of[9], 71), 0),
        "new_count": draw_new_count(jax.random.fold_in(key_of[9], 71), 0),
        "page_map": jax.random.permutation(key_of[8], TOTAL_PAGES).astype(jnp.int32),
    }


NEGATIVE_LIMIT = -1e30


def lookup(values_table, entry_ids):
    matches = entry_ids[..., None] == jnp.arange(values_table.shape[0], dtype=jnp.int32)
    return jnp.sum(jnp.where(matches, values_table, 0), axis=-1).astype(jnp.int32)


def token_info(row_ids, new_tok, prefix_len, new_count):
    request = row_ids // new_tok
    offset = row_ids - request * new_tok
    position = lookup(prefix_len, request) + offset
    is_valid = offset < lookup(new_count, request)
    return request, position, is_valid


def slot_info(page_ids, pages_req, prefix_len):
    request = page_ids // pages_req
    first_pos = (page_ids - request * pages_req) * PAGE_SLOTS
    position = (first_pos[:, None] + jnp.arange(PAGE_SLOTS, dtype=jnp.int32)[None, :]).reshape(-1)
    request = jnp.broadcast_to(request[:, None], (page_ids.shape[0], PAGE_SLOTS)).reshape(-1)
    is_live = position < lookup(prefix_len, request)
    return request, position, is_live


def permitted(query_meta, key_meta):
    query_req, query_pos, query_ok = query_meta
    key_req, key_pos, key_live = key_meta
    same = query_req[:, None] == key_req[None, :]
    causal = key_pos[None, :] <= query_pos[:, None]
    return same & causal & key_live[None, :] & query_ok[:, None]


def attend_head(query_rows, query_meta, cached_key_rows, cached_value_rows, cache_meta, own_key_rows, own_value_rows, own_meta):
    factor = HEAD_WIDTH ** -0.5
    highest = lax.Precision.HIGHEST
    query_f = query_rows.astype(jnp.float32)
    score_cache = jnp.einsum("qrd,kd->qrk", query_f, cached_key_rows.astype(jnp.float32), precision=highest) * factor
    score_own = jnp.einsum("qrd,kd->qrk", query_f, own_key_rows.astype(jnp.float32), precision=highest) * factor
    allow_cache = permitted(query_meta, cache_meta)[:, None, :]
    allow_own = permitted(query_meta, own_meta)[:, None, :]
    peak = jnp.maximum(jnp.max(jnp.where(allow_cache, score_cache, NEGATIVE_LIMIT), axis=-1),
                       jnp.max(jnp.where(allow_own, score_own, NEGATIVE_LIMIT), axis=-1))
    weight_cache = jnp.exp(jnp.where(allow_cache, score_cache - peak[..., None], NEGATIVE_LIMIT))
    weight_own = jnp.exp(jnp.where(allow_own, score_own - peak[..., None], NEGATIVE_LIMIT))
    total = jnp.sum(weight_cache, axis=-1) + jnp.sum(weight_own, axis=-1)
    rounded_cache = weight_cache.astype(jnp.bfloat16).astype(jnp.float32)
    rounded_own = weight_own.astype(jnp.bfloat16).astype(jnp.float32)
    numer = jnp.einsum("qrk,kd->qrd", rounded_cache, cached_value_rows.astype(jnp.float32), precision=highest)
    numer = numer + jnp.einsum("qrk,kd->qrd", rounded_own, own_value_rows.astype(jnp.float32), precision=highest)
    kept = jnp.maximum(total, 1.0)
    return numer / kept[..., None], peak + jnp.log(kept)


def reference(queries, rotated_new_keys, fresh_token_values, paged_key_cache, paged_value_cache, out_weight, prefix_len, new_count, page_map):
    query_tokens = queries.shape[0]
    new_tok = query_tokens // REQS
    pages_req = page_map.shape[0] // REQS
    row_ids = jnp.arange(query_tokens, dtype=jnp.int32)
    query_meta = token_info(row_ids, new_tok, prefix_len, new_count)
    query_head_rows = jnp.moveaxis(queries.reshape(query_tokens, KEY_VALUE_HEADS, QUERY_GROUP, HEAD_WIDTH), 1, 0)
    cached_key_rows = paged_key_cache.reshape(N_CTX, PAGES_PER_INDEX * PAGE_SLOTS, KEY_VALUE_HEADS, HEAD_WIDTH)
    cached_value_rows = paged_value_cache.reshape(N_CTX, PAGES_PER_INDEX * PAGE_SLOTS, KEY_VALUE_HEADS, HEAD_WIDTH)
    own_key_rows = rotated_new_keys.reshape(N_CTX, TOKENS_PER_INDEX, KEY_VALUE_HEADS, HEAD_WIDTH)
    own_value_rows = fresh_token_values.reshape(N_CTX, TOKENS_PER_INDEX, KEY_VALUE_HEADS, HEAD_WIDTH)
    page_sets = page_map.reshape(N_CTX, PAGES_PER_INDEX)
    set_ids = jnp.arange(N_CTX, dtype=jnp.int32)

    def absorb(running, inputs):
        keys_set, values_set, keys_own, values_own, page_ids, set_index = inputs
        cache_meta = slot_info(page_ids, pages_req, prefix_len)
        own_rows = set_index * TOKENS_PER_INDEX + jnp.arange(TOKENS_PER_INDEX, dtype=jnp.int32)
        own_meta = token_info(own_rows, new_tok, prefix_len, new_count)

        def per_head(args):
            head_q, head_k, head_v, head_ok, head_ov = args
            return attend_head(head_q, query_meta, head_k, head_v, cache_meta, head_ok, head_ov, own_meta)

        partial_value, log_total = lax.map(per_head, (query_head_rows, jnp.moveaxis(keys_set, 1, 0), jnp.moveaxis(values_set, 1, 0),
                                                jnp.moveaxis(keys_own, 1, 0), jnp.moveaxis(values_own, 1, 0)))
        run_peak, run_total, run_acc = running
        peak = jnp.maximum(run_peak, log_total)
        older = jnp.exp(run_peak - peak)
        fresh = jnp.exp(log_total - peak)
        return (peak, run_total * older + fresh, run_acc * older[..., None] + fresh[..., None] * partial_value), None

    initial_state = (jnp.full((KEY_VALUE_HEADS, query_tokens, QUERY_GROUP), NEGATIVE_LIMIT, jnp.float32),
                   jnp.zeros((KEY_VALUE_HEADS, query_tokens, QUERY_GROUP), jnp.float32),
                   jnp.zeros((KEY_VALUE_HEADS, query_tokens, QUERY_GROUP, HEAD_WIDTH), jnp.float32))
    (peak, total, accum), _ = lax.scan(absorb, initial_state, (cached_key_rows, cached_value_rows, own_key_rows, own_value_rows, page_sets, set_ids))
    attn = jnp.moveaxis(accum / total[..., None], 0, 1).reshape(query_tokens, QUERY_HEADS * HEAD_WIDTH).astype(jnp.bfloat16)
    return jnp.dot(attn, out_weight, preferred_element_type=jnp.float32).astype(jnp.bfloat16)
```

```python
import functools
import math

import jax
import jax.numpy as jnp
from jax import lax
from jax.experimental import pallas as pl
from jax.experimental.pallas import tpu as pltpu
from jax.sharding import PartitionSpec as P

NY, NZ, NC = 2, 8, 2
HEAD = 128
GROUP = 16
HEADS = GROUP // NC
PAGE = 128
PAGES = 12
TOKENS = 16
BLOCK = TOKENS * NC
ROWS = BLOCK * NZ
PAGES_REQ = 192
HALF = HEADS * HEAD
WIDE = HALF + 128
TILE = 4
KEYS = TILE * PAGE
SLOTS = 56
KV_ROWS = 2 * PAGES * PAGE + 2 * TOKENS
MASKED = -1e30
FLOOR = -1e29
SCALE = HEAD**-0.5 * math.log2(math.e)
OFFSETS = (0, 1, -1, 2, -2, 3, -3, 4)
BF = jnp.bfloat16
F32 = jnp.float32
VMEM = pl.BlockSpec(memory_space=pltpu.VMEM)
SMEM = pl.BlockSpec(memory_space=pltpu.SMEM)


def place(i):
    return i // (NZ * NC), (i // NC) % NZ, i % NC


def moved(x, dy=0, dz=0, dc=0):
    pairs = []
    for i in range(NY * NZ * NC):
        y, z, c = place(i)
        pairs.append((i, (((y + dy) % NY) * NZ + (z + dz) % NZ) * NC + (c + dc) % NC))
    return lax.ppermute(x, "ctx", pairs)


def near(block):
    return [moved(block, dz=d) for d in OFFSETS[1:5]]


def far(got):
    return [moved(got[2], dz=1), moved(got[3], dz=-1), moved(got[2], dz=2)]


def attend_kernel(page_map, prefix_len, new_count, *refs):
    q_refs, kv_refs, out_refs = refs[:NZ], refs[NZ : NZ + 4], refs[NZ + 4 : 2 * NZ + 4]
    keys, values, q_all, acc, peak, part_k, part_v = refs[2 * NZ + 4 :]
    me = lax.axis_index("ctx")
    y, z, c = place(me)
    prefix = prefix_len[y]
    fresh = new_count[y]
    ones = jnp.ones((PAGE, HEAD), BF)

    def store(slot, key, value):
        at = pl.ds(pl.multiple_of(slot * PAGE, PAGE), PAGE)
        keys[at, :] = key
        values[at, :HEAD] = value
        values[at, HEAD:] = ones

    carry = (jnp.int32(0), jnp.int32(0))
    for s, ref in enumerate(kv_refs):
        oy, oc = (y + s // 2) % NY, (c + s % 2) % NC
        base = ((oy * NZ + z) * NC + oc) * PAGES

        def visit(i, carry, ref=ref, base=base):
            count, edge = carry
            page = page_map[base + i]
            request = (page >= PAGES_REQ).astype(jnp.int32)
            live = prefix - (page - request * PAGES_REQ) * PAGE
            mine = request == y
            whole = mine & (live >= PAGE)
            some = mine & (live > 0) & (live < PAGE)
            at_k = pl.ds(pl.multiple_of(i * PAGE, PAGE), PAGE)
            at_v = pl.ds(pl.multiple_of((PAGES + i) * PAGE, PAGE), PAGE)

            @pl.when(whole)
            def _():
                store(count, ref[at_k, :], ref[at_v, :])

            @pl.when(some)
            def _():
                part_k[...] = ref[at_k, :]
                part_v[...] = ref[at_v, :]

            return count + whole.astype(jnp.int32), jnp.where(some, live, edge)

        carry = lax.fori_loop(0, PAGES, visit, carry)
    full, edge = carry
    has_edge = (edge > 0).astype(jnp.int32)
    new_slot = full + has_edge
    total = new_slot + 1

    @pl.when(edge > 0)
    def _():
        store(full, part_k[...], part_v[...])

    zero = jnp.zeros((PAGE, HEAD), BF)
    for k in range(TILE):
        store(new_slot + k, zero, zero)
    first, second = kv_refs[0], kv_refs[1]
    at0 = pl.multiple_of(new_slot * PAGE, PAGE)
    row = 2 * PAGES * PAGE
    for ref, core in ((first, c), (second, 1 - c)):
        at = pl.ds(pl.multiple_of(at0 + core * TOKENS, TOKENS), TOKENS)
        keys[at, :] = ref[row : row + TOKENS, :]
        values[at, :HEAD] = ref[row + TOKENS : row + 2 * TOKENS, :]

    for h in range(HEADS):
        for k in range(NZ):
            q_all[h, k * BLOCK : (k + 1) * BLOCK, :] = q_refs[k][:, h * HEAD : (h + 1) * HEAD]
    acc[...] = jnp.zeros(acc.shape, F32)
    peak[...] = jnp.full(peak.shape, FLOOR, F32)

    offset = jnp.concatenate(
        [
            lax.rem(z - d + NZ, NZ) * BLOCK + lax.broadcasted_iota(jnp.int32, (BLOCK, PAGE), 0)
            for d in OFFSETS
        ],
        axis=0,
    )
    lane = lax.broadcasted_iota(jnp.int32, (ROWS, PAGE), 1)
    key_offset = z * BLOCK + lane
    new_limit = jnp.where((lane < BLOCK) & (key_offset < fresh), key_offset, 2 * ROWS)
    new_ok = (new_limit <= offset).astype(jnp.int32)

    def visit_tile(heads, masked, t, _):
        at = pl.ds(pl.multiple_of(t * KEYS, KEYS), KEYS)
        kt = keys[at, :]
        vt = values[at, :]
        allowed = []
        if masked:
            for k in range(TILE):
                slot = t * TILE + k
                limit = jnp.where(slot < full, PAGE, jnp.where(slot < new_slot, edge, 0))
                cached = (lane < limit).astype(jnp.int32)
                allowed.append(jnp.where(slot == new_slot, new_ok, cached) > 0)
        for h in heads:
            s = lax.dot_general(q_all[h], kt, (((1,), (1,)), ((), ())), preferred_element_type=F32)
            parts = [s[:, k * PAGE : (k + 1) * PAGE] for k in range(TILE)]
            if masked:
                parts = [jnp.where(a, p, MASKED) for a, p in zip(allowed, parts)]
            top = functools.reduce(jnp.maximum, parts)
            old = peak[h]
            new = jnp.maximum(old, jnp.max(top, axis=1, keepdims=True))
            shift = new * SCALE
            w = jnp.concatenate([jnp.exp2(p * SCALE - shift).astype(BF) for p in parts], axis=1)
            alpha = jnp.exp2((old - new) * SCALE)
            more = jnp.dot(w, vt, preferred_element_type=F32)
            acc[h] = acc[h] * jnp.concatenate([alpha, alpha], axis=1) + more
            peak[h] = new
        return 0

    whole_tiles = full // TILE
    tiles = (total + TILE - 1) // TILE
    for g in range(0, HEADS, 4):
        heads = range(g, g + 4)
        lax.fori_loop(0, whole_tiles, functools.partial(visit_tile, heads, False), 0)
        lax.fori_loop(whole_tiles, tiles, functools.partial(visit_tile, heads, True), 0)

    logs = jnp.zeros((ROWS, PAGE), F32)
    for h in range(HEADS):
        weight = acc[h, :, HEAD:]
        kept = jnp.maximum(weight, 1.0)
        out = (acc[h, :, :HEAD] / kept).astype(BF)
        log_total = jnp.where(weight > 0, peak[h] * SCALE + jnp.log(kept) * math.log2(math.e), MASKED)
        high = log_total.astype(BF).astype(F32)
        rest = log_total - high
        mid = rest.astype(BF).astype(F32)
        low = rest - mid
        logs = jnp.where(lane == h, high, logs)
        logs = jnp.where(lane == HEADS + h, mid, logs)
        logs = jnp.where(lane == 2 * HEADS + h, low, logs)
        for k in range(NZ):
            out_refs[k][:, h * HEAD : (h + 1) * HEAD] = out[k * BLOCK : (k + 1) * BLOCK, :]
    logs = logs.astype(BF)
    for k in range(NZ):
        out_refs[k][:, HALF:] = logs[k * BLOCK : (k + 1) * BLOCK, :]


def attend(page_map, prefix_len, new_count, q_blocks, kv):
    return pl.pallas_call(
        attend_kernel,
        out_shape=[jax.ShapeDtypeStruct((BLOCK, WIDE), BF)] * NZ,
        in_specs=[SMEM] * 3 + [VMEM] * (NZ + 4),
        out_specs=[VMEM] * NZ,
        scratch_shapes=[
            pltpu.VMEM((SLOTS * PAGE, HEAD), BF),
            pltpu.VMEM((SLOTS * PAGE, 2 * HEAD), BF),
            pltpu.VMEM((HEADS, ROWS, HEAD), BF),
            pltpu.VMEM((HEADS, ROWS, 2 * HEAD), F32),
            pltpu.VMEM((HEADS, ROWS, PAGE), F32),
            pltpu.VMEM((PAGE, HEAD), BF),
            pltpu.VMEM((PAGE, HEAD), BF),
        ],
        compiler_params=pltpu.CompilerParams(vmem_limit_bytes=40 * 2**20),
        cost_estimate=pl.CostEstimate(
            flops=4 * HEADS * ROWS * 24 * PAGE * HEAD, bytes_accessed=6 * 2**20, transcendentals=HEADS * ROWS * 24 * PAGE
        ),
        name="attend",
    )(page_map, prefix_len, new_count, *q_blocks, *kv)


def merge_kernel(new_count, *refs):
    blocks, out = refs[:NZ], refs[NZ]
    y, z, _ = place(lax.axis_index("ctx"))
    logs = []
    for ref in blocks:
        part = ref[:, HALF:].astype(F32)
        logs.append(part + pltpu.roll(part, PAGE - HEADS, 1) + pltpu.roll(part, PAGE - 2 * HEADS, 1))
    top = functools.reduce(jnp.maximum, logs)
    weights = [jnp.exp2(g - top) for g in logs]
    total = functools.reduce(jnp.add, weights)
    offset = z * BLOCK + lax.broadcasted_iota(jnp.int32, (BLOCK, PAGE), 0)
    scale = jnp.where(offset < new_count[y], 1.0 / total, 0.0)
    weights = [w * scale for w in weights]
    for h in range(HEADS):
        at = slice(h * HEAD, (h + 1) * HEAD)
        terms = [ref[:, at].astype(F32) * w[:, h : h + 1] for ref, w in zip(blocks, weights)]
        out[:, at] = functools.reduce(jnp.add, terms).astype(BF)


def merge(new_count, blocks):
    return pl.pallas_call(
        merge_kernel,
        out_shape=jax.ShapeDtypeStruct((BLOCK, HALF), BF),
        in_specs=[SMEM] + [VMEM] * NZ,
        out_specs=VMEM,
        cost_estimate=pl.CostEstimate(flops=2**20, bytes_accessed=2**20, transcendentals=0),
        name="merge",
    )(new_count, *blocks)


def project_kernel(*refs):
    pieces, weight, out, rows = refs[:8], refs[8], refs[9], refs[10]
    y, z, c = place(lax.axis_index("ctx"))
    for s in range(4):
        request, half = (y + s // 2) % NY, (c + s % 2) % NC
        columns = pl.ds(pl.multiple_of(half * HALF, HALF), HALF)
        for k, d in enumerate(OFFSETS):
            ref, first = (pieces[2 * s], 0) if k < 5 else (pieces[2 * s + 1], 5)
            at = pl.multiple_of(request * ROWS + lax.rem(z - d + NZ, NZ) * BLOCK, BLOCK)
            rows[pl.ds(at, BLOCK), columns] = ref[(k - first) * BLOCK : (k - first + 1) * BLOCK, :]
    for r in range(0, NY * ROWS, 256):
        out[r : r + 256, :] = jnp.dot(rows[r : r + 256, :], weight[...], preferred_element_type=F32).astype(BF)


def project(pieces, weight):
    tokens, depth, columns = NY * ROWS, NC * HALF, weight.shape[1]
    return pl.pallas_call(
        project_kernel,
        out_shape=jax.ShapeDtypeStruct((tokens, columns), BF),
        in_specs=[VMEM] * 9,
        out_specs=VMEM,
        scratch_shapes=[pltpu.VMEM((tokens, depth), BF)],
        compiler_params=pltpu.CompilerParams(vmem_limit_bytes=24 * 2**20),
        cost_estimate=pl.CostEstimate(flops=2 * tokens * depth * columns, bytes_accessed=5 * 2**20, transcendentals=0),
        name="project",
    )(*pieces, weight)


def local(
    queries,
    rotated_new_keys,
    fresh_token_values,
    paged_key_cache,
    paged_value_cache,
    out_weight,
    prefix_len,
    new_count,
    page_map,
):
    c = lax.axis_index("ctx") % NC
    slots = PAGES * PAGE
    kv_own = jnp.concatenate(
        [paged_key_cache.reshape(slots, HEAD), paged_value_cache.reshape(slots, HEAD), rotated_new_keys, fresh_token_values]
    )
    kv_other = moved(kv_own, dy=1)
    left, right = queries[:, :HALF], queries[:, HALF:]
    keep = jnp.where(c == 0, left, right)
    got = moved(jnp.where(c == 0, right, left), dc=1)
    block = jnp.where(c == 0, jnp.concatenate([keep, got]), jnp.concatenate([got, keep]))
    q_near = near(block)
    q_blocks = [block] + q_near + far(q_near)
    kv = [kv_own, moved(kv_own, dc=1), kv_other, moved(kv_other, dc=1)]
    parts = attend(page_map, prefix_len, new_count, q_blocks, kv)
    back = [parts[0]] + [moved(parts[k], dz=-OFFSETS[k]) for k in (7, 5, 6, 3, 4, 1, 2)]
    attn = merge(new_count, back)
    a_near = near(attn)
    first = jnp.concatenate([attn] + a_near)
    second = jnp.concatenate(far(a_near))
    first_y, second_y = moved(first, dy=1), moved(second, dy=1)
    pieces = []
    for one, two in ((first, second), (first_y, second_y)):
        pieces += [one, two, moved(one, dc=1), moved(two, dc=1)]
    terms = project(pieces, out_weight)
    tp = lax.axis_size("tp")
    terms = terms.reshape(tp, terms.shape[0] // tp, terms.shape[1])
    swapped = lax.all_to_all(terms, "tp", split_axis=0, concat_axis=0, tiled=True)
    return jnp.sum(swapped.astype(F32), axis=0).astype(BF)


def solution(mesh):
    placed = (
        P("ctx", "tp"),
        P("ctx", "tp"),
        P("ctx", "tp"),
        P("ctx", None, "tp"),
        P("ctx", None, "tp"),
        P("tp", "ctx"),
        P(),
        P(),
        P(),
    )
    return jax.shard_map(local, mesh=mesh, in_specs=placed, out_specs=P("tp", "ctx"), check_vma=False)
```

```python
import functools
import math

import jax
import jax.numpy as jnp
from jax import lax
from jax.experimental import pallas as pl
from jax.experimental.pallas import tpu as pltpu
from jax.sharding import PartitionSpec as P

NY, NZ, NC = 2, 8, 2
HEAD = 128
GROUP = 16
HEADS = GROUP // NC
PAGE = 128
PAGES = 12
TOKENS = 16
BLOCK = TOKENS * NC
ROWS = BLOCK * NZ
PAGES_REQ = 192
HALF = HEADS * HEAD
WIDE = HALF + 128
TILE = 4
STACK = 1
KEYS = TILE * PAGE
SLOTS = 52
KV_ROWS = 2 * PAGES * PAGE + 2 * TOKENS
MASKED = -1e30
FLOOR = -1e29
SAFE = 100.0
SCALE = HEAD**-0.5 * math.log2(math.e)
OFFSETS = (0, 1, -1, 2, -2, 3, -3, 4)
BF = jnp.bfloat16
F32 = jnp.float32
VMEM = pl.BlockSpec(memory_space=pltpu.VMEM)
SMEM = pl.BlockSpec(memory_space=pltpu.SMEM)


def place(i):
    return i // (NZ * NC), (i // NC) % NZ, i % NC


def moved(x, dy=0, dz=0, dc=0):
    pairs = []
    for i in range(NY * NZ * NC):
        y, z, c = place(i)
        pairs.append((i, (((y + dy) % NY) * NZ + (z + dz) % NZ) * NC + (c + dc) % NC))
    return lax.ppermute(x, "ctx", pairs)


def near(block):
    return [moved(block, dz=d) for d in OFFSETS[1:5]]


def far(got):
    got = lax.optimization_barrier(got)
    return [moved(got[2], dz=1), moved(got[3], dz=-1), moved(got[2], dz=2)]


def largest_square(rows):
    x = rows.astype(F32)
    return jnp.max(jnp.sum(x * x, axis=1, keepdims=True), axis=0, keepdims=True)


def pack_kernel(k, v, new_k, new_v, out, sems):
    slots = PAGES * PAGE
    half = slots // 2
    pieces = [(k, i * half, i * half, half) for i in range(2)]
    pieces += [(v, i * half, slots + i * half, half) for i in range(2)]
    pieces += [(new_k, 0, 2 * slots, TOKENS), (new_v, 0, 2 * slots + TOKENS, TOKENS)]
    copies = [
        pltpu.make_async_copy(ref.at[pl.ds(start, n)], out.at[pl.ds(to, n)], sems.at[i])
        for i, (ref, start, to, n) in enumerate(pieces)
    ]
    for copy in copies:
        copy.start()
    for copy in copies:
        copy.wait()
    square = jnp.maximum(largest_square(out[:slots, :]), largest_square(out[2 * slots : 2 * slots + TOKENS, :]))
    out[KV_ROWS:, :] = jnp.broadcast_to(square * 1.01, (TOKENS, HEAD)).astype(BF)


def pack(k, v, new_k, new_v):
    return pl.pallas_call(
        pack_kernel,
        out_shape=jax.ShapeDtypeStruct((KV_ROWS + TOKENS, HEAD), BF),
        in_specs=[pl.BlockSpec(memory_space=pltpu.HBM)] * 4,
        out_specs=VMEM,
        scratch_shapes=[pltpu.SemaphoreType.DMA((6,))],
        compiler_params=pltpu.CompilerParams(vmem_limit_bytes=60 * 2**20),
        cost_estimate=pl.CostEstimate(flops=0, bytes_accessed=2 * KV_ROWS * HEAD * 2, transcendentals=0),
        name="pack",
    )(k, v, new_k, new_v)


def sort_kernel(page_map, prefix_len, new_count, *refs):
    kv_refs, (keys, values, info, square), (part_k, part_v) = refs[:4], refs[4:8], refs[8:]
    y, z, c = place(lax.axis_index("ctx"))
    prefix = prefix_len[y]

    def span(slot):
        return pl.ds(pl.multiple_of(slot * PAGE, PAGE), PAGE)

    def store(slot, key, value):
        keys[span(slot), :] = key
        values[span(slot), :] = value

    carry = (jnp.int32(0), jnp.int32(0))
    for s, ref in enumerate(kv_refs):
        oy, oc = (y + s // 2) % NY, (c + s % 2) % NC
        base = ((oy * NZ + z) * NC + oc) * PAGES

        def visit(i, carry, ref=ref, base=base):
            count, edge = carry
            page = page_map[base + i]
            request = (page >= PAGES_REQ).astype(jnp.int32)
            live = prefix - (page - request * PAGES_REQ) * PAGE
            mine = request == y
            whole = mine & (live >= PAGE)
            some = mine & (live > 0) & (live < PAGE)

            @pl.when(whole)
            def _():
                store(count, ref[span(i), :], ref[span(PAGES + i), :])

            @pl.when(some)
            def _():
                part_k[...] = ref[span(i), :]
                part_v[...] = ref[span(PAGES + i), :]

            return count + whole.astype(jnp.int32), jnp.where(some, live, edge)

        carry = lax.fori_loop(0, PAGES, visit, carry)
    full, edge = carry
    new_slot = full + (edge > 0).astype(jnp.int32)
    info[0] = full
    info[1] = edge
    info[2] = new_slot
    info[3] = new_count[y]

    @pl.when(edge > 0)
    def _():
        store(full, part_k[...], part_v[...])

    zero = jnp.zeros((PAGE, HEAD), BF)
    for k in range(1, TILE):
        store(new_slot + k, zero, zero)
    row = 2 * PAGES * PAGE
    first, second = kv_refs[0], kv_refs[1]
    swap = c > 0

    def fresh_rows(start):
        a, b = first[start : start + TOKENS, :], second[start : start + TOKENS, :]
        rows = [jnp.where(swap, b, a), jnp.where(swap, a, b)]
        return jnp.concatenate(rows + [jnp.zeros((PAGE - BLOCK, HEAD), BF)], axis=0)

    store(new_slot, fresh_rows(row), fresh_rows(row + TOKENS))
    square[...] = functools.reduce(jnp.maximum, [ref[KV_ROWS:, :].astype(F32) for ref in kv_refs])


def sort_pages(page_map, prefix_len, new_count, kv):
    pages = jax.ShapeDtypeStruct((SLOTS * PAGE, HEAD), BF)
    return pl.pallas_call(
        sort_kernel,
        out_shape=[pages, pages, jax.ShapeDtypeStruct((4,), jnp.int32), jax.ShapeDtypeStruct((TOKENS, HEAD), F32)],
        in_specs=[SMEM] * 3 + [VMEM] * 4,
        out_specs=[VMEM, VMEM, SMEM, VMEM],
        scratch_shapes=[pltpu.VMEM((PAGE, HEAD), BF)] * 2,
        compiler_params=pltpu.CompilerParams(vmem_limit_bytes=12 * 2**20),
        cost_estimate=pl.CostEstimate(flops=0, bytes_accessed=6 * 2**20, transcendentals=0),
        name="sort_pages",
    )(page_map, prefix_len, new_count, *kv)


def attend_kernel(offsets, info, *refs):
    n = len(offsets)
    rows = n * BLOCK
    q_refs, (keys, values, square), out_refs = refs[:n], refs[n : n + 3], refs[n + 3 : 2 * n + 3]
    q_all, acc, peak = refs[2 * n + 3 :]
    _, z, _ = place(lax.axis_index("ctx"))
    full, edge, new_slot, fresh = info[0], info[1], info[2], info[3]

    for h in range(HEADS):
        for k in range(n):
            at = slice(h * rows + k * BLOCK, h * rows + (k + 1) * BLOCK)
            q_all[at, :] = q_refs[k][:, h * HEAD : (h + 1) * HEAD]
    acc[...] = jnp.zeros(acc.shape, F32)
    limit2 = jnp.max(largest_square(q_all[...]) * (SCALE * SCALE) * jnp.max(square[...]))
    small = limit2 <= SAFE * SAFE
    peak[...] = jnp.full(peak.shape, jnp.where(small, 0.0, FLOOR), F32)

    lane = lax.broadcasted_iota(jnp.int32, (rows, PAGE), 1)
    offset = jnp.concatenate(
        [
            lax.rem(z - d + NZ, NZ) * BLOCK + lax.broadcasted_iota(jnp.int32, (BLOCK, PAGE), 0)
            for d in offsets
        ],
        axis=0,
    )
    key_offset = z * BLOCK + lane
    new_limit = jnp.where((lane < BLOCK) & (key_offset < fresh), key_offset, 2 * ROWS)
    new_ok = (new_limit <= offset).astype(jnp.int32)
    ones = jnp.ones((KEYS, HEAD), BF)

    def visit_tile(masked, shifted, t, _):
        at = pl.ds(pl.multiple_of(t * KEYS, KEYS), KEYS)
        kt = keys[at, :]
        vt = jnp.concatenate([values[at, :], ones], axis=1)
        allowed = []
        if masked:
            for k in range(TILE):
                slot = t * TILE + k
                limit = jnp.where(slot < full, PAGE, jnp.where(slot < new_slot, edge, 0))
                cached = (lane < limit).astype(jnp.int32)
                allowed.append(jnp.concatenate([jnp.where(slot == new_slot, new_ok, cached)] * STACK, axis=0) > 0)
        for g in range(0, HEADS * rows, STACK * rows):
            at = slice(g, g + STACK * rows)
            s = lax.dot_general(q_all[at, :], kt, (((1,), (1,)), ((), ())), preferred_element_type=F32)
            parts = [s[:, k * PAGE : (k + 1) * PAGE] for k in range(TILE)]
            if masked:
                parts = [jnp.where(a, p, MASKED) for a, p in zip(allowed, parts)]
            if shifted:
                top = functools.reduce(jnp.maximum, parts)
                old = peak[at, :]
                new = jnp.maximum(old, jnp.max(top, axis=1, keepdims=True))
                shift = new * SCALE
                w = jnp.concatenate([jnp.exp2(p * SCALE - shift).astype(BF) for p in parts], axis=1)
                alpha = jnp.exp2((old - new) * SCALE)
                more = jnp.dot(w, vt, preferred_element_type=F32)
                acc[at, :] = acc[at, :] * jnp.concatenate([alpha, alpha], axis=1) + more
                peak[at, :] = new
            else:
                w = jnp.concatenate([jnp.exp2(p * SCALE).astype(BF) for p in parts], axis=1)
                acc[at, :] = acc[at, :] + jnp.dot(w, vt, preferred_element_type=F32)
        return 0

    whole_tiles = full // TILE
    tiles = (new_slot + TILE) // TILE

    def visit_all(shifted):
        lax.fori_loop(0, whole_tiles, functools.partial(visit_tile, False, shifted), 0)
        lax.fori_loop(whole_tiles, tiles, functools.partial(visit_tile, True, shifted), 0)

    pl.when(small)(functools.partial(visit_all, False))
    pl.when(jnp.logical_not(small))(functools.partial(visit_all, True))

    logs = jnp.zeros((rows, PAGE), F32)
    for h in range(HEADS):
        at = slice(h * rows, (h + 1) * rows)
        weight = acc[at, HEAD:]
        kept = jnp.where(weight > 0, weight, 1.0)
        out = (acc[at, :HEAD] / kept).astype(BF)
        log_total = jnp.where(weight > 0, peak[at, :] * SCALE + jnp.log(kept) * math.log2(math.e), MASKED)
        high = log_total.astype(BF).astype(F32)
        rest = log_total - high
        mid = rest.astype(BF).astype(F32)
        for place_at, part in enumerate((high, mid, rest - mid)):
            logs = jnp.where(lane == place_at * HEADS + h, part, logs)
        for k in range(n):
            out_refs[k][:, h * HEAD : (h + 1) * HEAD] = out[k * BLOCK : (k + 1) * BLOCK, :]
    logs = logs.astype(BF)
    for k in range(n):
        out_refs[k][:, HALF:] = logs[k * BLOCK : (k + 1) * BLOCK, :]


def attend(offsets, info, q_blocks, keys, values, square):
    n = len(offsets)
    rows = n * BLOCK
    return pl.pallas_call(
        functools.partial(attend_kernel, offsets),
        out_shape=[jax.ShapeDtypeStruct((BLOCK, WIDE), BF)] * n,
        in_specs=[SMEM] + [VMEM] * (n + 3),
        out_specs=[VMEM] * n,
        scratch_shapes=[
            pltpu.VMEM((HEADS * rows, HEAD), BF),
            pltpu.VMEM((HEADS * rows, 2 * HEAD), F32),
            pltpu.VMEM((HEADS * rows, PAGE), F32),
        ],
        compiler_params=pltpu.CompilerParams(vmem_limit_bytes=16 * 2**20),
        cost_estimate=pl.CostEstimate(
            flops=4 * HEADS * rows * 24 * PAGE * HEAD, bytes_accessed=4 * 2**20, transcendentals=HEADS * rows * 24 * PAGE
        ),
        name="attend",
    )(info, *q_blocks, keys, values, square)


def merge_kernel(new_count, *refs):
    blocks, out = refs[:NZ], refs[NZ]
    y, z, _ = place(lax.axis_index("ctx"))
    logs = []
    for ref in blocks:
        part = ref[:, HALF:].astype(F32)
        logs.append(part + pltpu.roll(part, PAGE - HEADS, 1) + pltpu.roll(part, PAGE - 2 * HEADS, 1))
    top = functools.reduce(jnp.maximum, logs)
    weights = [jnp.exp2(g - top) for g in logs]
    total = functools.reduce(jnp.add, weights)
    offset = z * BLOCK + lax.broadcasted_iota(jnp.int32, (BLOCK, PAGE), 0)
    scale = jnp.where(offset < new_count[y], 1.0 / total, 0.0)
    weights = [w * scale for w in weights]
    for h in range(HEADS):
        at = slice(h * HEAD, (h + 1) * HEAD)
        terms = [ref[:, at].astype(F32) * w[:, h : h + 1] for ref, w in zip(blocks, weights)]
        out[:, at] = functools.reduce(jnp.add, terms).astype(BF)


def merge(new_count, blocks):
    return pl.pallas_call(
        merge_kernel,
        out_shape=jax.ShapeDtypeStruct((BLOCK, HALF), BF),
        in_specs=[SMEM] + [VMEM] * NZ,
        out_specs=VMEM,
        compiler_params=pltpu.CompilerParams(vmem_limit_bytes=4 * 2**20),
        cost_estimate=pl.CostEstimate(flops=2**20, bytes_accessed=2**20, transcendentals=0),
        name="merge",
    )(new_count, *blocks)


def project_kernel(*refs):
    pieces, weight, out, rows = refs[:8], refs[8], refs[9], refs[10]
    y, z, c = place(lax.axis_index("ctx"))
    for s in range(4):
        request, half = (y + s // 2) % NY, (c + s % 2) % NC
        columns = pl.ds(pl.multiple_of(half * HALF, HALF), HALF)
        for k, d in enumerate(OFFSETS):
            ref, first = (pieces[2 * s], 0) if k < 5 else (pieces[2 * s + 1], 5)
            at = pl.multiple_of(request * ROWS + lax.rem(z - d + NZ, NZ) * BLOCK, BLOCK)
            rows[pl.ds(at, BLOCK), columns] = ref[(k - first) * BLOCK : (k - first + 1) * BLOCK, :]
    for r in range(0, NY * ROWS, 256):
        out[r : r + 256, :] = jnp.dot(rows[r : r + 256, :], weight[...], preferred_element_type=F32).astype(BF)


def project(pieces, weight):
    tokens, depth, columns = NY * ROWS, NC * HALF, weight.shape[1]
    return pl.pallas_call(
        project_kernel,
        out_shape=jax.ShapeDtypeStruct((tokens, columns), BF),
        in_specs=[VMEM] * 9,
        out_specs=VMEM,
        scratch_shapes=[pltpu.VMEM((tokens, depth), BF)],
        compiler_params=pltpu.CompilerParams(vmem_limit_bytes=12 * 2**20),
        cost_estimate=pl.CostEstimate(flops=2 * tokens * depth * columns, bytes_accessed=5 * 2**20, transcendentals=0),
        name="project",
    )(*pieces, weight)


def local(
    queries,
    rotated_new_keys,
    fresh_token_values,
    paged_key_cache,
    paged_value_cache,
    out_weight,
    prefix_len,
    new_count,
    page_map,
):
    c = lax.axis_index("ctx") % NC
    slots = PAGES * PAGE
    kv_own = pack(
        paged_key_cache.reshape(slots, HEAD), paged_value_cache.reshape(slots, HEAD), rotated_new_keys, fresh_token_values
    )
    kv_own, queries = lax.optimization_barrier((kv_own, queries))
    kv_other = moved(kv_own, dy=1)
    left, right = queries[:, :HALF], queries[:, HALF:]
    keep = jnp.where(c == 0, left, right)
    got = moved(jnp.where(c == 0, right, left), dc=1)
    block = jnp.where(c == 0, jnp.concatenate([keep, got]), jnp.concatenate([got, keep]))
    q_near = near(block)
    q_far = far(q_near)
    kv_other, q_far = lax.optimization_barrier((kv_other, q_far))
    q_blocks = [block] + q_near + q_far
    kv = [kv_own, moved(kv_own, dc=1), kv_other, moved(kv_other, dc=1)]
    keys, values, info, square = sort_pages(page_map, prefix_len, new_count, kv)
    parts = attend(OFFSETS, info, q_blocks, keys, values, square)
    back = [parts[0]] + [moved(parts[k], dz=-OFFSETS[k]) for k in (7, 5, 6, 3, 4, 1, 2)]
    attn = merge(new_count, back)
    a_near = near(attn)
    first = jnp.concatenate([attn] + a_near)
    second = jnp.concatenate(far(a_near))
    first_y, second_y = moved(first, dy=1), moved(second, dy=1)
    pieces = []
    for one, two in ((first, second), (first_y, second_y)):
        pieces += [one, two, moved(one, dc=1), moved(two, dc=1)]
    terms = project(pieces, out_weight)
    tp = lax.axis_size("tp")
    terms = terms.reshape(tp, terms.shape[0] // tp, terms.shape[1])
    swapped = lax.all_to_all(terms, "tp", split_axis=0, concat_axis=0, tiled=True)
    return jnp.sum(swapped.astype(F32), axis=0).astype(BF)


def solution(mesh):
    placed = (
        P("ctx", "tp"),
        P("ctx", "tp"),
        P("ctx", "tp"),
        P("ctx", None, "tp"),
        P("ctx", None, "tp"),
        P("tp", "ctx"),
        P(),
        P(),
        P(),
    )
    return jax.shard_map(local, mesh=mesh, in_specs=placed, out_specs=P("tp", "ctx"), check_vma=False)
```

```python
import functools
import math

import jax
import jax.numpy as jnp
from jax import lax
from jax.experimental import pallas as pl
from jax.experimental.pallas import tpu as pltpu
from jax.sharding import PartitionSpec as P

NY, NZ, NC = 2, 8, 2
HEAD = 128
GROUP = 16
HEADS = GROUP // NC
PAGE = 128
PAGES = 12
TOKENS = 16
BLOCK = TOKENS * NC
ROWS = BLOCK * NZ
PAGES_REQ = 192
HALF = HEADS * HEAD
WIDE = HALF + 128
TILE = 4
STACK = 1
KEYS = TILE * PAGE
SLOTS = 56
NEAR_SLOTS = 26
KV_ROWS = 2 * PAGES * PAGE + 2 * TOKENS
MASKED = -1e30
FLOOR = -1e29
SAFE = 100.0
SCALE = HEAD**-0.5 * math.log2(math.e)
OFFSETS = (0, 1, -1, 2, -2, 3, -3, 4)
BF = jnp.bfloat16
F32 = jnp.float32
VMEM = pl.BlockSpec(memory_space=pltpu.VMEM)
SMEM = pl.BlockSpec(memory_space=pltpu.SMEM)


def place(i):
    return i // (NZ * NC), (i // NC) % NZ, i % NC


def moved(x, dy=0, dz=0, dc=0):
    pairs = []
    for i in range(NY * NZ * NC):
        y, z, c = place(i)
        pairs.append((i, (((y + dy) % NY) * NZ + (z + dz) % NZ) * NC + (c + dc) % NC))
    return lax.ppermute(x, "ctx", pairs)


def near(block):
    return [moved(block, dz=d) for d in OFFSETS[1:5]]


def far(got, first=()):
    got, first = lax.optimization_barrier((got, first))
    return [moved(got[2], dz=1), moved(got[3], dz=-1), moved(got[2], dz=2)], first


def largest_square(rows):
    x = rows.astype(F32)
    sums = jnp.dot((x * x).astype(BF), jnp.ones((HEAD, HEAD), BF), preferred_element_type=F32)
    return jnp.max(sums, axis=0, keepdims=True) * 1.01


def pack_kernel(k, v, new_k, new_v, out, sems):
    slots = PAGES * PAGE
    half = slots // 2
    pieces = [(k, i * half, i * half, half) for i in range(2)]
    pieces += [(v, i * half, slots + i * half, half) for i in range(2)]
    pieces += [(new_k, 0, 2 * slots, TOKENS), (new_v, 0, 2 * slots + TOKENS, TOKENS)]
    copies = [
        pltpu.make_async_copy(ref.at[pl.ds(start, n)], out.at[pl.ds(to, n)], sems.at[i])
        for i, (ref, start, to, n) in enumerate(pieces)
    ]
    for copy in copies:
        copy.start()
    for copy in copies:
        copy.wait()
    square = jnp.maximum(largest_square(out[:slots, :]), largest_square(out[2 * slots : 2 * slots + TOKENS, :]))
    out[KV_ROWS:, :] = jnp.broadcast_to(square * 1.01, (TOKENS, HEAD)).astype(BF)


def pack(k, v, new_k, new_v):
    return pl.pallas_call(
        pack_kernel,
        out_shape=jax.ShapeDtypeStruct((KV_ROWS + TOKENS, HEAD), BF),
        in_specs=[pl.BlockSpec(memory_space=pltpu.HBM)] * 4,
        out_specs=VMEM,
        scratch_shapes=[pltpu.SemaphoreType.DMA((6,))],
        compiler_params=pltpu.CompilerParams(vmem_limit_bytes=60 * 2**20),
        cost_estimate=pl.CostEstimate(flops=0, bytes_accessed=2 * KV_ROWS * HEAD * 2, transcendentals=0),
        name="pack",
    )(k, v, new_k, new_v)


def sort_kernel(far_side, ints, *refs):
    if far_side:
        before, keys_in, values_in, square_in = refs[:4]
        refs = refs[4:]
    kv_refs, (keys, values, info, square) = refs[:2], refs[2:]
    y, z, c = place(lax.axis_index("ctx"))
    prefix = ints[NY * PAGES_REQ + y]

    def span(slot):
        return pl.ds(pl.multiple_of(slot * PAGE, PAGE), PAGE)

    def store(slot, key, value):
        keys[span(slot), :] = key
        values[span(slot), :] = value

    zero = jnp.zeros((PAGE, HEAD), BF)
    if far_side:
        held = slice(0, NEAR_SLOTS * PAGE)
        keys[held, :] = keys_in[held, :]
        values[held, :] = values_in[held, :]
        carry = (before[0], before[1])
    else:
        row = 2 * PAGES * PAGE
        swap = c > 0

        def fresh_rows(start):
            a, b = (ref[start : start + TOKENS, :] for ref in kv_refs)
            rows = [jnp.where(swap, b, a), jnp.where(swap, a, b)]
            return jnp.concatenate(rows + [jnp.zeros((PAGE - BLOCK, HEAD), BF)], axis=0)

        store(0, fresh_rows(row), fresh_rows(row + TOKENS))
        store(1, zero, zero)
        carry = (jnp.int32(0), jnp.int32(0))
    for s, ref in enumerate(kv_refs):
        oy, oc = (y + far_side) % NY, (c + s) % NC
        base = ((oy * NZ + z) * NC + oc) * PAGES

        def visit(i, carry, ref=ref, base=base):
            count, edge = carry
            page = ints[base + i]
            request = (page >= PAGES_REQ).astype(jnp.int32)
            live = prefix - (page - request * PAGES_REQ) * PAGE
            mine = request == y
            whole = mine & (live >= PAGE)
            some = mine & (live > 0) & (live < PAGE)

            @pl.when(whole | some)
            def _():
                store(jnp.where(whole, count + 2, 1), ref[span(i), :], ref[span(PAGES + i), :])

            return count + whole.astype(jnp.int32), jnp.where(some, live, edge)

        carry = lax.fori_loop(0, PAGES, visit, carry)
    full, edge = carry
    largest = [ref[KV_ROWS:, :].astype(F32) for ref in kv_refs]
    if far_side:
        largest.append(square_in[...])
        for k in range(TILE - 1):
            store(full + 2 + k, zero, zero)
    info[0] = full
    info[1] = edge
    info[2] = ints[NY * PAGES_REQ + NY + y]
    square[...] = functools.reduce(jnp.maximum, largest)


def sort_pages(far_side, ints, kv, before=()):
    slots = SLOTS if far_side else NEAR_SLOTS
    pages = jax.ShapeDtypeStruct((slots * PAGE, HEAD), BF)
    operands = []
    if before:
        keys, values, info, square = before
        operands = [info, keys, values, square]
    return pl.pallas_call(
        functools.partial(sort_kernel, far_side),
        out_shape=[pages, pages, jax.ShapeDtypeStruct((4,), jnp.int32), jax.ShapeDtypeStruct((TOKENS, HEAD), F32)],
        in_specs=([SMEM] * 2 + [VMEM] * 3 if before else [SMEM]) + [VMEM] * 2,
        out_specs=[VMEM, VMEM, SMEM, VMEM],
        compiler_params=pltpu.CompilerParams(vmem_limit_bytes=12 * 2**20),
        cost_estimate=pl.CostEstimate(flops=0, bytes_accessed=2**20, transcendentals=0),
        name="sort_pages",
    )(ints, *operands, *kv)


def gather_kernel(*refs):
    q_refs, (q_all, square) = refs[:NZ], refs[NZ:]
    for h in range(HEADS):
        for k in range(NZ):
            at = slice(h * ROWS + k * BLOCK, h * ROWS + (k + 1) * BLOCK)
            q_all[at, :] = q_refs[k][:, h * HEAD : (h + 1) * HEAD]
    square[0] = jnp.max(largest_square(q_all[...])) * (SCALE * SCALE)


def gather_rows(q_blocks):
    return pl.pallas_call(
        gather_kernel,
        out_shape=[jax.ShapeDtypeStruct((HEADS * ROWS, HEAD), BF), jax.ShapeDtypeStruct((1,), F32)],
        in_specs=[VMEM] * NZ,
        out_specs=[VMEM, SMEM],
        compiler_params=pltpu.CompilerParams(vmem_limit_bytes=8 * 2**20),
        cost_estimate=pl.CostEstimate(flops=0, bytes_accessed=2**20, transcendentals=0),
        name="gather_rows",
    )(*q_blocks)


def attend_kernel(info, q_square, q_all, keys, values, square, *refs):
    out_refs, (acc, peak) = refs[:NZ], refs[NZ:]
    _, z, _ = place(lax.axis_index("ctx"))
    full, edge, fresh = info[0], info[1], info[2]
    total = full + 2
    acc[...] = jnp.zeros(acc.shape, F32)
    small = q_square[0] * jnp.max(square[...]) <= SAFE * SAFE
    peak[...] = jnp.full(peak.shape, jnp.where(small, 0.0, FLOOR), F32)
    lane = lax.broadcasted_iota(jnp.int32, (ROWS, PAGE), 1)
    offset = jnp.concatenate(
        [
            lax.rem(z - d + NZ, NZ) * BLOCK + lax.broadcasted_iota(jnp.int32, (BLOCK, PAGE), 0)
            for d in OFFSETS
        ],
        axis=0,
    )
    key_offset = z * BLOCK + lane
    new_limit = jnp.where((lane < BLOCK) & (key_offset < fresh), key_offset, 2 * ROWS)
    new_ok = (new_limit <= offset).astype(jnp.int32)
    ones = jnp.ones((KEYS, HEAD), BF)

    def visit_tile(masked, shifted, t, _):
        at = pl.ds(pl.multiple_of(t * KEYS, KEYS), KEYS)
        kt = keys[at, :]
        vt = jnp.concatenate([values[at, :], ones], axis=1)
        allowed = []
        if masked:
            for k in range(TILE):
                slot = t * TILE + k
                limit = jnp.where(slot == 1, edge, jnp.where(slot < total, PAGE, 0))
                cached = (lane < limit).astype(jnp.int32)
                allowed.append(jnp.concatenate([jnp.where(slot == 0, new_ok, cached)] * STACK, axis=0) > 0)
        for g in range(0, HEADS * ROWS, STACK * ROWS):
            at = slice(g, g + STACK * ROWS)
            s = lax.dot_general(q_all[at, :], kt, (((1,), (1,)), ((), ())), preferred_element_type=F32)
            parts = [s[:, k * PAGE : (k + 1) * PAGE] for k in range(TILE)]
            if masked:
                parts = [jnp.where(a, p, MASKED) for a, p in zip(allowed, parts)]
            if shifted:
                top = functools.reduce(jnp.maximum, parts)
                old = peak[at, :]
                new = jnp.maximum(old, jnp.max(top, axis=1, keepdims=True))
                shift = new * SCALE
                w = jnp.concatenate([jnp.exp2(p * SCALE - shift).astype(BF) for p in parts], axis=1)
                alpha = jnp.exp2((old - new) * SCALE)
                more = jnp.dot(w, vt, preferred_element_type=F32)
                acc[at, :] = acc[at, :] * jnp.concatenate([alpha, alpha], axis=1) + more
                peak[at, :] = new
            else:
                w = jnp.concatenate([jnp.exp2(p * SCALE).astype(BF) for p in parts], axis=1)
                acc[at, :] = acc[at, :] + jnp.dot(w, vt, preferred_element_type=F32)
        return 0

    whole_tiles = total // TILE
    tiles = (total + TILE - 1) // TILE

    def visit_all(shifted):
        last = jnp.maximum(whole_tiles, 1)
        lax.fori_loop(0, 1, functools.partial(visit_tile, True, shifted), 0)
        lax.fori_loop(1, last, functools.partial(visit_tile, False, shifted), 0)
        lax.fori_loop(last, tiles, functools.partial(visit_tile, True, shifted), 0)

    pl.when(small)(functools.partial(visit_all, False))
    pl.when(jnp.logical_not(small))(functools.partial(visit_all, True))

    logs = jnp.zeros((ROWS, PAGE), F32)
    for h in range(HEADS):
        at = slice(h * ROWS, (h + 1) * ROWS)
        weight = acc[at, HEAD:]
        kept = jnp.where(weight > 0, weight, 1.0)
        out = (acc[at, :HEAD] / kept).astype(BF)
        log_total = jnp.where(weight > 0, peak[at, :] * SCALE + jnp.log(kept) * math.log2(math.e), MASKED)
        high = log_total.astype(BF).astype(F32)
        rest = log_total - high
        mid = rest.astype(BF).astype(F32)
        for place_at, part in enumerate((high, mid, rest - mid)):
            logs = jnp.where(lane == place_at * HEADS + h, part, logs)
        for k in range(NZ):
            out_refs[k][:, h * HEAD : (h + 1) * HEAD] = out[k * BLOCK : (k + 1) * BLOCK, :]
    logs = logs.astype(BF)
    for k in range(NZ):
        out_refs[k][:, HALF:] = logs[k * BLOCK : (k + 1) * BLOCK, :]


def attend(info, q_square, q_all, keys, values, square):
    total = HEADS * ROWS
    return pl.pallas_call(
        attend_kernel,
        out_shape=[jax.ShapeDtypeStruct((BLOCK, WIDE), BF)] * NZ,
        in_specs=[SMEM] * 2 + [VMEM] * 4,
        out_specs=[VMEM] * NZ,
        scratch_shapes=[pltpu.VMEM((total, 2 * HEAD), F32), pltpu.VMEM((total, PAGE), F32)],
        compiler_params=pltpu.CompilerParams(vmem_limit_bytes=16 * 2**20),
        cost_estimate=pl.CostEstimate(
            flops=4 * total * 24 * PAGE * HEAD, bytes_accessed=4 * 2**20, transcendentals=total * 24 * PAGE
        ),
        name="attend",
    )(info, q_square, q_all, keys, values, square)


def merge_kernel(new_count, *refs):
    blocks, out = refs[:NZ], refs[NZ]
    y, z, _ = place(lax.axis_index("ctx"))
    logs = []
    for ref in blocks:
        part = ref[:, HALF:].astype(F32)
        logs.append(part + pltpu.roll(part, PAGE - HEADS, 1) + pltpu.roll(part, PAGE - 2 * HEADS, 1))
    top = functools.reduce(jnp.maximum, logs)
    weights = [jnp.exp2(g - top) for g in logs]
    total = functools.reduce(jnp.add, weights)
    offset = z * BLOCK + lax.broadcasted_iota(jnp.int32, (BLOCK, PAGE), 0)
    scale = jnp.where(offset < new_count[y], 1.0 / total, 0.0)
    weights = [w * scale for w in weights]
    for h in range(HEADS):
        at = slice(h * HEAD, (h + 1) * HEAD)
        terms = [ref[:, at].astype(F32) * w[:, h : h + 1] for ref, w in zip(blocks, weights)]
        out[:, at] = functools.reduce(jnp.add, terms).astype(BF)


def merge(new_count, blocks):
    return pl.pallas_call(
        merge_kernel,
        out_shape=jax.ShapeDtypeStruct((BLOCK, HALF), BF),
        in_specs=[SMEM] + [VMEM] * NZ,
        out_specs=VMEM,
        compiler_params=pltpu.CompilerParams(vmem_limit_bytes=4 * 2**20),
        cost_estimate=pl.CostEstimate(flops=2**20, bytes_accessed=2**20, transcendentals=0),
        name="merge",
    )(new_count, *blocks)


def project_kernel(*refs):
    pieces, weight, out, rows = refs[:8], refs[8], refs[9], refs[10]
    y, z, c = place(lax.axis_index("ctx"))
    for s in range(4):
        request, half = (y + s // 2) % NY, (c + s % 2) % NC
        columns = pl.ds(pl.multiple_of(half * HALF, HALF), HALF)
        for k, d in enumerate(OFFSETS):
            ref, first = (pieces[2 * s], 0) if k < 5 else (pieces[2 * s + 1], 5)
            at = pl.multiple_of(request * ROWS + lax.rem(z - d + NZ, NZ) * BLOCK, BLOCK)
            rows[pl.ds(at, BLOCK), columns] = ref[(k - first) * BLOCK : (k - first + 1) * BLOCK, :]
    for r in range(0, NY * ROWS, 256):
        out[r : r + 256, :] = jnp.dot(rows[r : r + 256, :], weight[...], preferred_element_type=F32).astype(BF)


def project(pieces, weight):
    tokens, depth, columns = NY * ROWS, NC * HALF, weight.shape[1]
    return pl.pallas_call(
        project_kernel,
        out_shape=jax.ShapeDtypeStruct((tokens, columns), BF),
        in_specs=[VMEM] * 9,
        out_specs=VMEM,
        scratch_shapes=[pltpu.VMEM((tokens, depth), BF)],
        compiler_params=pltpu.CompilerParams(vmem_limit_bytes=12 * 2**20),
        cost_estimate=pl.CostEstimate(flops=2 * tokens * depth * columns, bytes_accessed=5 * 2**20, transcendentals=0),
        name="project",
    )(*pieces, weight)


def local(
    queries,
    rotated_new_keys,
    fresh_token_values,
    paged_key_cache,
    paged_value_cache,
    out_weight,
    prefix_len,
    new_count,
    page_map,
):
    c = lax.axis_index("ctx") % NC
    slots = PAGES * PAGE
    left, right = queries[:, :HALF], queries[:, HALF:]
    keep, send = jnp.where(c == 0, left, right), jnp.where(c == 0, right, left)
    send, new_keys = lax.optimization_barrier((send, rotated_new_keys))
    got = moved(send, dc=1)
    kv_own = pack(
        paged_key_cache.reshape(slots, HEAD), paged_value_cache.reshape(slots, HEAD), new_keys, fresh_token_values
    )
    kv_own, got = lax.optimization_barrier((kv_own, got))
    kv_other = moved(kv_own, dy=1)
    block = jnp.where(c == 0, jnp.concatenate([keep, got]), jnp.concatenate([got, keep]))
    q_near = near(block)
    q_far, _ = far(q_near)
    ints = jnp.concatenate([page_map, prefix_len, new_count])
    kv_mine, q_near = lax.optimization_barrier(([kv_own, moved(kv_own, dc=1), ints], q_near))
    *kv_mine, ints = kv_mine
    sorted_near = sort_pages(0, ints, kv_mine)
    kv_other, q_far, sorted_near = lax.optimization_barrier((kv_other, q_far, sorted_near))
    kv_far = [kv_other, moved(kv_other, dc=1)]
    q_all, q_square = gather_rows([block] + q_near + q_far)
    kv_far, q_all = lax.optimization_barrier((kv_far, q_all))
    keys, values, info, square = sort_pages(1, ints, kv_far, sorted_near)
    parts = attend(info, q_square, q_all, keys, values, square)
    back = [parts[0]] + [moved(parts[k], dz=-OFFSETS[k]) for k in (7, 5, 6, 3, 4, 1, 2)]
    attn = merge(new_count, back)
    a_near = near(attn)
    a_far, _ = far(a_near)
    first, second = jnp.concatenate([attn] + a_near), jnp.concatenate(a_far)
    pieces = []
    for one, two in ((first, second), (moved(first, dy=1), moved(second, dy=1))):
        pieces += [one, two, moved(one, dc=1), moved(two, dc=1)]
    terms = project(pieces, out_weight)
    tp = lax.axis_size("tp")
    terms = terms.reshape(tp, terms.shape[0] // tp, terms.shape[1])
    swapped = lax.all_to_all(terms, "tp", split_axis=0, concat_axis=0, tiled=True)
    return jnp.sum(swapped.astype(F32), axis=0).astype(BF)


def solution(mesh):
    placed = (
        P("ctx", "tp"),
        P("ctx", "tp"),
        P("ctx", "tp"),
        P("ctx", None, "tp"),
        P("ctx", None, "tp"),
        P("tp", "ctx"),
        P(),
        P(),
        P(),
    )
    return jax.shard_map(local, mesh=mesh, in_specs=placed, out_specs=P("tp", "ctx"), check_vma=False)
```

```python
import functools
import math

import jax
import jax.numpy as jnp
from jax import lax
from jax.experimental import pallas as pl
from jax.experimental.pallas import tpu as pltpu
from jax.sharding import PartitionSpec as P

NY, NZ, NC = 2, 8, 2
HEAD = 128
GROUP = 16
HEADS = GROUP // NC
PAGE = 128
PAGES = 12
TOKENS = 16
BLOCK = TOKENS * NC
ROWS = BLOCK * NZ
PAGES_REQ = 192
HALF = HEADS * HEAD
WIDE = HALF + 128
TILE = 4
STACK = 1
KEYS = TILE * PAGE
SLOTS = 56
NEAR_SLOTS = 26
KV_ROWS = 2 * PAGES * PAGE + 2 * TOKENS
MASKED = -1e30
FLOOR = -1e29
SAFE = 100.0
SCALE = HEAD**-0.5 * math.log2(math.e)
OFFSETS = (0, 1, -1, 2, -2, 3, -3, 4)
BF = jnp.bfloat16
F32 = jnp.float32
VMEM = pl.BlockSpec(memory_space=pltpu.VMEM)
SMEM = pl.BlockSpec(memory_space=pltpu.SMEM)


def place(i):
    return i // (NZ * NC), (i // NC) % NZ, i % NC


def moved(x, dy=0, dz=0, dc=0):
    pairs = []
    for i in range(NY * NZ * NC):
        y, z, c = place(i)
        pairs.append((i, (((y + dy) % NY) * NZ + (z + dz) % NZ) * NC + (c + dc) % NC))
    return lax.ppermute(x, "ctx", pairs)


def near(block):
    return [moved(block, dz=d) for d in OFFSETS[1:5]]


def far(got, first=()):
    got, first = lax.optimization_barrier((got, first))
    return [moved(got[2], dz=1), moved(got[3], dz=-1), moved(got[2], dz=2)], first


def largest_square(rows):
    x = rows.astype(F32)
    sums = jnp.dot((x * x).astype(BF), jnp.ones((HEAD, HEAD), BF), preferred_element_type=F32)
    return jnp.max(sums, axis=0, keepdims=True) * 1.01


def pack_kernel(k, v, new_k, new_v, out, sems):
    slots = PAGES * PAGE
    half = slots // 2
    pieces = [(k, i * half, i * half, half) for i in range(2)]
    pieces += [(v, i * half, slots + i * half, half) for i in range(2)]
    pieces += [(new_k, 0, 2 * slots, TOKENS), (new_v, 0, 2 * slots + TOKENS, TOKENS)]
    copies = [
        pltpu.make_async_copy(ref.at[pl.ds(start, n)], out.at[pl.ds(to, n)], sems.at[i])
        for i, (ref, start, to, n) in enumerate(pieces)
    ]
    for copy in copies:
        copy.start()
    for copy in copies:
        copy.wait()
    square = jnp.maximum(largest_square(out[:slots, :]), largest_square(out[2 * slots : 2 * slots + TOKENS, :]))
    out[KV_ROWS:, :] = jnp.broadcast_to(square * 1.01, (TOKENS, HEAD)).astype(BF)


def pack(k, v, new_k, new_v):
    return pl.pallas_call(
        pack_kernel,
        out_shape=jax.ShapeDtypeStruct((KV_ROWS + TOKENS, HEAD), BF),
        in_specs=[pl.BlockSpec(memory_space=pltpu.HBM)] * 4,
        out_specs=VMEM,
        scratch_shapes=[pltpu.SemaphoreType.DMA((6,))],
        compiler_params=pltpu.CompilerParams(vmem_limit_bytes=60 * 2**20),
        cost_estimate=pl.CostEstimate(flops=0, bytes_accessed=2 * KV_ROWS * HEAD * 2, transcendentals=0),
        name="pack",
    )(k, v, new_k, new_v)


def sort_kernel(far_side, ints, *refs):
    if far_side:
        before, keys_in, values_in, square_in = refs[:4]
        refs = refs[4:]
    kv_refs, (keys, values, info, square) = refs[:2], refs[2:]
    y, z, c = place(lax.axis_index("ctx"))
    prefix = ints[NY * PAGES_REQ + y]

    def span(slot):
        return pl.ds(pl.multiple_of(slot * PAGE, PAGE), PAGE)

    def store(slot, key, value):
        keys[span(slot), :] = key
        values[span(slot), :] = value

    zero = jnp.zeros((PAGE, HEAD), BF)
    if far_side:
        held = slice(0, NEAR_SLOTS * PAGE)
        keys[held, :] = keys_in[held, :]
        values[held, :] = values_in[held, :]
        carry = (before[0], before[1])
    else:
        row = 2 * PAGES * PAGE
        swap = c > 0

        def fresh_rows(start):
            a, b = (ref[start : start + TOKENS, :] for ref in kv_refs)
            rows = [jnp.where(swap, b, a), jnp.where(swap, a, b)]
            return jnp.concatenate(rows + [jnp.zeros((PAGE - BLOCK, HEAD), BF)], axis=0)

        store(0, fresh_rows(row), fresh_rows(row + TOKENS))
        store(1, zero, zero)
        carry = (jnp.int32(0), jnp.int32(0))
    for s, ref in enumerate(kv_refs):
        oy, oc = (y + far_side) % NY, (c + s) % NC
        base = ((oy * NZ + z) * NC + oc) * PAGES

        def visit(i, carry, ref=ref, base=base):
            count, edge = carry
            page = ints[base + i]
            request = (page >= PAGES_REQ).astype(jnp.int32)
            live = prefix - (page - request * PAGES_REQ) * PAGE
            mine = request == y
            whole = mine & (live >= PAGE)
            some = mine & (live > 0) & (live < PAGE)

            @pl.when(whole | some)
            def _():
                store(jnp.where(whole, count + 2, 1), ref[span(i), :], ref[span(PAGES + i), :])

            return count + whole.astype(jnp.int32), jnp.where(some, live, edge)

        carry = lax.fori_loop(0, PAGES, visit, carry)
    full, edge = carry
    largest = [ref[KV_ROWS:, :].astype(F32) for ref in kv_refs]
    if far_side:
        largest.append(square_in[...])
        for k in range(TILE - 1):
            store(full + 2 + k, zero, zero)
    info[0] = full
    info[1] = edge
    info[2] = ints[NY * PAGES_REQ + NY + y]
    square[...] = functools.reduce(jnp.maximum, largest)


def sort_pages(far_side, ints, kv, before=()):
    slots = SLOTS if far_side else NEAR_SLOTS
    pages = jax.ShapeDtypeStruct((slots * PAGE, HEAD), BF)
    operands = []
    if before:
        keys, values, info, square = before
        operands = [info, keys, values, square]
    return pl.pallas_call(
        functools.partial(sort_kernel, far_side),
        out_shape=[pages, pages, jax.ShapeDtypeStruct((4,), jnp.int32), jax.ShapeDtypeStruct((TOKENS, HEAD), F32)],
        in_specs=([SMEM] * 2 + [VMEM] * 3 if before else [SMEM]) + [VMEM] * 2,
        out_specs=[VMEM, VMEM, SMEM, VMEM],
        compiler_params=pltpu.CompilerParams(vmem_limit_bytes=12 * 2**20),
        cost_estimate=pl.CostEstimate(flops=0, bytes_accessed=2**20, transcendentals=0),
        name="sort_pages",
    )(ints, *operands, *kv)


def gather_kernel(*refs):
    q_refs, (q_all, square) = refs[:NZ], refs[NZ:]
    for h in range(HEADS):
        for k in range(NZ):
            at = slice(h * ROWS + k * BLOCK, h * ROWS + (k + 1) * BLOCK)
            q_all[at, :] = q_refs[k][:, h * HEAD : (h + 1) * HEAD]
    square[0] = jnp.max(largest_square(q_all[...])) * (SCALE * SCALE)


def gather_rows(q_blocks):
    return pl.pallas_call(
        gather_kernel,
        out_shape=[jax.ShapeDtypeStruct((HEADS * ROWS, HEAD), BF), jax.ShapeDtypeStruct((1,), F32)],
        in_specs=[VMEM] * NZ,
        out_specs=[VMEM, SMEM],
        compiler_params=pltpu.CompilerParams(vmem_limit_bytes=8 * 2**20),
        cost_estimate=pl.CostEstimate(flops=0, bytes_accessed=2**20, transcendentals=0),
        name="gather_rows",
    )(*q_blocks)


def attend_kernel(info, q_square, q_all, keys, values, square, *refs):
    out_refs, (acc, peak) = refs[:NZ], refs[NZ:]
    _, z, _ = place(lax.axis_index("ctx"))
    full, edge, fresh = info[0], info[1], info[2]
    total = full + 2
    acc[...] = jnp.zeros(acc.shape, F32)
    small = q_square[0] * jnp.max(square[...]) <= SAFE * SAFE
    peak[...] = jnp.full(peak.shape, jnp.where(small, 0.0, FLOOR), F32)
    lane = lax.broadcasted_iota(jnp.int32, (ROWS, PAGE), 1)
    offset = jnp.concatenate(
        [
            lax.rem(z - d + NZ, NZ) * BLOCK + lax.broadcasted_iota(jnp.int32, (BLOCK, PAGE), 0)
            for d in OFFSETS
        ],
        axis=0,
    )
    key_offset = z * BLOCK + lane
    new_limit = jnp.where((lane < BLOCK) & (key_offset < fresh), key_offset, 2 * ROWS)
    new_ok = (new_limit <= offset).astype(jnp.int32)
    ones = jnp.ones((KEYS, HEAD), BF)

    def visit_tile(masked, shifted, t, _):
        at = pl.ds(pl.multiple_of(t * KEYS, KEYS), KEYS)
        kt = keys[at, :]
        vt = jnp.concatenate([values[at, :], ones], axis=1)
        allowed = []
        if masked:
            for k in range(TILE):
                slot = t * TILE + k
                limit = jnp.where(slot == 1, edge, jnp.where(slot < total, PAGE, 0))
                cached = (lane < limit).astype(jnp.int32)
                allowed.append(jnp.concatenate([jnp.where(slot == 0, new_ok, cached)] * STACK, axis=0) > 0)
        for g in range(0, HEADS * ROWS, STACK * ROWS):
            at = slice(g, g + STACK * ROWS)
            s = lax.dot_general(q_all[at, :], kt, (((1,), (1,)), ((), ())), preferred_element_type=F32)
            parts = [s[:, k * PAGE : (k + 1) * PAGE] for k in range(TILE)]
            if masked:
                parts = [jnp.where(a, p, MASKED) for a, p in zip(allowed, parts)]
            if shifted:
                top = functools.reduce(jnp.maximum, parts)
                old = peak[at, :]
                new = jnp.maximum(old, jnp.max(top, axis=1, keepdims=True))
                shift = new * SCALE
                w = jnp.concatenate([jnp.exp2(p * SCALE - shift).astype(BF) for p in parts], axis=1)
                alpha = jnp.exp2((old - new) * SCALE)
                more = jnp.dot(w, vt, preferred_element_type=F32)
                acc[at, :] = acc[at, :] * jnp.concatenate([alpha, alpha], axis=1) + more
                peak[at, :] = new
            else:
                w = jnp.concatenate([jnp.exp2(p * SCALE).astype(BF) for p in parts], axis=1)
                acc[at, :] = acc[at, :] + jnp.dot(w, vt, preferred_element_type=F32)
        return 0

    whole_tiles = total // TILE
    tiles = (total + TILE - 1) // TILE

    def visit_all(shifted):
        last = jnp.maximum(whole_tiles, 1)
        lax.fori_loop(0, 1, functools.partial(visit_tile, True, shifted), 0)
        lax.fori_loop(1, last, functools.partial(visit_tile, False, shifted), 0)
        lax.fori_loop(last, tiles, functools.partial(visit_tile, True, shifted), 0)

    pl.when(small)(functools.partial(visit_all, False))
    pl.when(jnp.logical_not(small))(functools.partial(visit_all, True))

    logs = jnp.zeros((ROWS, PAGE), F32)
    for h in range(HEADS):
        at = slice(h * ROWS, (h + 1) * ROWS)
        weight = acc[at, HEAD:]
        kept = jnp.where(weight > 0, weight, 1.0)
        out = (acc[at, :HEAD] / kept).astype(BF)
        log_total = jnp.where(weight > 0, peak[at, :] * SCALE + jnp.log(kept) * math.log2(math.e), MASKED)
        high = log_total.astype(BF).astype(F32)
        rest = log_total - high
        mid = rest.astype(BF).astype(F32)
        for place_at, part in enumerate((high, mid, rest - mid)):
            logs = jnp.where(lane == place_at * HEADS + h, part, logs)
        for k in range(NZ):
            out_refs[k][:, h * HEAD : (h + 1) * HEAD] = out[k * BLOCK : (k + 1) * BLOCK, :]
    logs = logs.astype(BF)
    for k in range(NZ):
        out_refs[k][:, HALF:] = logs[k * BLOCK : (k + 1) * BLOCK, :]


def attend(info, q_square, q_all, keys, values, square):
    total = HEADS * ROWS
    return pl.pallas_call(
        attend_kernel,
        out_shape=[jax.ShapeDtypeStruct((BLOCK, WIDE), BF)] * NZ,
        in_specs=[SMEM] * 2 + [VMEM] * 4,
        out_specs=[VMEM] * NZ,
        scratch_shapes=[pltpu.VMEM((total, 2 * HEAD), F32), pltpu.VMEM((total, PAGE), F32)],
        compiler_params=pltpu.CompilerParams(vmem_limit_bytes=16 * 2**20),
        cost_estimate=pl.CostEstimate(
            flops=4 * total * 24 * PAGE * HEAD, bytes_accessed=4 * 2**20, transcendentals=total * 24 * PAGE
        ),
        name="attend",
    )(info, q_square, q_all, keys, values, square)


def merge_kernel(new_count, *refs):
    blocks, out = refs[:NZ], refs[NZ]
    y, z, _ = place(lax.axis_index("ctx"))
    logs = []
    for ref in blocks:
        part = ref[:, HALF:].astype(F32)
        logs.append(part + pltpu.roll(part, PAGE - HEADS, 1) + pltpu.roll(part, PAGE - 2 * HEADS, 1))
    top = functools.reduce(jnp.maximum, logs)
    weights = [jnp.exp2(g - top) for g in logs]
    total = functools.reduce(jnp.add, weights)
    offset = z * BLOCK + lax.broadcasted_iota(jnp.int32, (BLOCK, PAGE), 0)
    scale = jnp.where(offset < new_count[y], 1.0 / total, 0.0)
    weights = [w * scale for w in weights]
    for h in range(HEADS):
        at = slice(h * HEAD, (h + 1) * HEAD)
        terms = [ref[:, at].astype(F32) * w[:, h : h + 1] for ref, w in zip(blocks, weights)]
        out[:, at] = functools.reduce(jnp.add, terms).astype(BF)


def merge(new_count, blocks):
    return pl.pallas_call(
        merge_kernel,
        out_shape=jax.ShapeDtypeStruct((BLOCK, HALF), BF),
        in_specs=[SMEM] + [VMEM] * NZ,
        out_specs=VMEM,
        compiler_params=pltpu.CompilerParams(vmem_limit_bytes=4 * 2**20),
        cost_estimate=pl.CostEstimate(flops=2**20, bytes_accessed=2**20, transcendentals=0),
        name="merge",
    )(new_count, *blocks)


def project_rows(pieces, weight, rows):
    _, z, c = place(lax.axis_index("ctx"))
    for s in range(NC):
        half = (c + s) % NC
        columns = pl.ds(pl.multiple_of(half * HALF, HALF), HALF)
        for k, d in enumerate(OFFSETS):
            ref, first = (pieces[2 * s], 0) if k < 5 else (pieces[2 * s + 1], 5)
            at = pl.multiple_of(lax.rem(z - d + NZ, NZ) * BLOCK, BLOCK)
            rows[pl.ds(at, BLOCK), columns] = ref[(k - first) * BLOCK : (k - first + 1) * BLOCK, :]
    return jnp.dot(rows[...], weight[...], preferred_element_type=F32).astype(BF)


def project_own_kernel(*refs):
    pieces, (weight, out, rows) = refs[:4], refs[4:]
    out[...] = project_rows(pieces, weight, rows)


def project_other_kernel(*refs):
    pieces, (weight, own, out, rows) = refs[:4], refs[4:]
    y, _, _ = place(lax.axis_index("ctx"))
    out[pl.ds(pl.multiple_of(y * ROWS, ROWS), ROWS), :] = own[...]
    out[pl.ds(pl.multiple_of((1 - y) * ROWS, ROWS), ROWS), :] = project_rows(pieces, weight, rows)


def project(kernel, name, rows, operands):
    depth, columns = operands[4].shape
    return pl.pallas_call(
        kernel,
        out_shape=jax.ShapeDtypeStruct((rows, columns), BF),
        in_specs=[VMEM] * len(operands),
        out_specs=VMEM,
        scratch_shapes=[pltpu.VMEM((ROWS, depth), BF)],
        compiler_params=pltpu.CompilerParams(vmem_limit_bytes=12 * 2**20),
        cost_estimate=pl.CostEstimate(flops=2 * ROWS * depth * columns, bytes_accessed=2**20, transcendentals=0),
        name=name,
    )(*operands)


def local(
    queries,
    rotated_new_keys,
    fresh_token_values,
    paged_key_cache,
    paged_value_cache,
    out_weight,
    prefix_len,
    new_count,
    page_map,
):
    c = lax.axis_index("ctx") % NC
    slots = PAGES * PAGE
    left, right = queries[:, :HALF], queries[:, HALF:]
    keep, send = jnp.where(c == 0, left, right), jnp.where(c == 0, right, left)
    send, new_keys = lax.optimization_barrier((send, rotated_new_keys))
    got = moved(send, dc=1)
    kv_own = pack(
        paged_key_cache.reshape(slots, HEAD), paged_value_cache.reshape(slots, HEAD), new_keys, fresh_token_values
    )
    kv_own, got = lax.optimization_barrier((kv_own, got))
    kv_other = moved(kv_own, dy=1)
    block = jnp.where(c == 0, jnp.concatenate([keep, got]), jnp.concatenate([got, keep]))
    q_near = near(block)
    q_far, _ = far(q_near)
    ints = jnp.concatenate([page_map, prefix_len, new_count])
    kv_mine, q_near = lax.optimization_barrier(([kv_own, moved(kv_own, dc=1), ints], q_near))
    *kv_mine, ints = kv_mine
    sorted_near = sort_pages(0, ints, kv_mine)
    kv_other, q_far, sorted_near = lax.optimization_barrier((kv_other, q_far, sorted_near))
    kv_far = [kv_other, moved(kv_other, dc=1)]
    q_all, q_square = gather_rows([block] + q_near + q_far)
    kv_far, q_all = lax.optimization_barrier((kv_far, q_all))
    keys, values, info, square = sort_pages(1, ints, kv_far, sorted_near)
    parts = attend(info, q_square, q_all, keys, values, square)
    back = [parts[0]] + [moved(parts[k], dz=-OFFSETS[k]) for k in (7, 5, 6, 3, 4, 1, 2)]
    attn = merge(new_count, back)
    a_near = near(attn)
    a_far, _ = far(a_near)
    first, second = jnp.concatenate([attn] + a_near), jnp.concatenate(a_far)
    own = [first, second, moved(first, dc=1), moved(second, dc=1)]
    first_y, second_y = moved(first, dy=1), moved(second, dy=1)
    other = [first_y, second_y, moved(first_y, dc=1), moved(second_y, dc=1)]
    terms = project(project_own_kernel, "project_own", ROWS, own + [out_weight])
    terms = project(project_other_kernel, "project_other", NY * ROWS, other + [out_weight, terms])
    tp = lax.axis_size("tp")
    terms = terms.reshape(tp, terms.shape[0] // tp, terms.shape[1])
    swapped = lax.all_to_all(terms, "tp", split_axis=0, concat_axis=0, tiled=True)
    return jnp.sum(swapped.astype(F32), axis=0).astype(BF)


def solution(mesh):
    placed = (
        P("ctx", "tp"),
        P("ctx", "tp"),
        P("ctx", "tp"),
        P("ctx", None, "tp"),
        P("ctx", None, "tp"),
        P("tp", "ctx"),
        P(),
        P(),
        P(),
    )
    return jax.shard_map(local, mesh=mesh, in_specs=placed, out_specs=P("tp", "ctx"), check_vma=False)
```

```python
import functools
import math

import jax
import jax.numpy as jnp
from jax import lax
from jax.experimental import pallas as pl
from jax.experimental.pallas import tpu as pltpu
from jax.sharding import PartitionSpec as P

NY, NZ, NC = 2, 8, 2
HEAD = 128
GROUP = 16
HEADS = GROUP // NC
PAGE = 128
PAGES = 12
TOKENS = 16
BLOCK = TOKENS * NC
ROWS = BLOCK * NZ
PAGES_REQ = 192
HALF = HEADS * HEAD
WIDE = HALF + 128
TILE = 4
STACK = 1
KEYS = TILE * PAGE
SLOTS = 56
NEAR_SLOTS = 26
KV_ROWS = 2 * PAGES * PAGE + 2 * TOKENS
MASKED = -1e30
FLOOR = -1e29
SAFE = 100.0
SCALE = HEAD**-0.5 * math.log2(math.e)
OFFSETS = (0, 1, -1, 2, -2, 3, -3, 4)
BF = jnp.bfloat16
F32 = jnp.float32
VMEM = pl.BlockSpec(memory_space=pltpu.VMEM)
SMEM = pl.BlockSpec(memory_space=pltpu.SMEM)


def place(i):
    return i // (NZ * NC), (i // NC) % NZ, i % NC


def moved(x, dy=0, dz=0, dc=0):
    pairs = []
    for i in range(NY * NZ * NC):
        y, z, c = place(i)
        pairs.append((i, (((y + dy) % NY) * NZ + (z + dz) % NZ) * NC + (c + dc) % NC))
    return lax.ppermute(x, "ctx", pairs)


def near(block):
    return [moved(block, dz=d) for d in OFFSETS[1:5]]


def far(got, first=()):
    got, first = lax.optimization_barrier((got, first))
    return [moved(got[2], dz=1), moved(got[3], dz=-1), moved(got[2], dz=2)], first


def largest_square(rows):
    x = rows.astype(F32)
    sums = jnp.dot((x * x).astype(BF), jnp.ones((HEAD, HEAD), BF), preferred_element_type=F32)
    return jnp.max(sums, axis=0, keepdims=True) * 1.01


def pack_kernel(k, v, new_k, new_v, out, sems):
    slots = PAGES * PAGE
    half = slots // 2
    pieces = [(k, i * half, i * half, half) for i in range(2)]
    pieces += [(v, i * half, slots + i * half, half) for i in range(2)]
    pieces += [(new_k, 0, 2 * slots, TOKENS), (new_v, 0, 2 * slots + TOKENS, TOKENS)]
    copies = [
        pltpu.make_async_copy(ref.at[pl.ds(start, n)], out.at[pl.ds(to, n)], sems.at[i])
        for i, (ref, start, to, n) in enumerate(pieces)
    ]
    for copy in copies:
        copy.start()
    for copy in copies:
        copy.wait()
    square = jnp.maximum(largest_square(out[:slots, :]), largest_square(out[2 * slots : 2 * slots + TOKENS, :]))
    out[KV_ROWS:, :] = jnp.broadcast_to(square * 1.01, (TOKENS, HEAD)).astype(BF)


def pack(k, v, new_k, new_v):
    return pl.pallas_call(
        pack_kernel,
        out_shape=jax.ShapeDtypeStruct((KV_ROWS + TOKENS, HEAD), BF),
        in_specs=[pl.BlockSpec(memory_space=pltpu.HBM)] * 4,
        out_specs=VMEM,
        scratch_shapes=[pltpu.SemaphoreType.DMA((6,))],
        compiler_params=pltpu.CompilerParams(vmem_limit_bytes=60 * 2**20),
        cost_estimate=pl.CostEstimate(flops=0, bytes_accessed=2 * KV_ROWS * HEAD * 2, transcendentals=0),
        name="pack",
    )(k, v, new_k, new_v)


def sort_kernel(far_side, ints, *refs):
    if far_side:
        before, keys_in, values_in, square_in = refs[:4]
        refs = refs[4:]
    kv_refs, (keys, values, info, square) = refs[:2], refs[2:]
    y, z, c = place(lax.axis_index("ctx"))
    prefix = ints[NY * PAGES_REQ + y]

    def span(slot):
        return pl.ds(pl.multiple_of(slot * PAGE, PAGE), PAGE)

    def store(slot, key, value):
        keys[span(slot), :] = key
        values[span(slot), :] = value

    zero = jnp.zeros((PAGE, HEAD), BF)
    if far_side:
        held = slice(0, NEAR_SLOTS * PAGE)
        keys[held, :] = keys_in[held, :]
        values[held, :] = values_in[held, :]
        carry = (before[0], before[1])
    else:
        row = 2 * PAGES * PAGE
        swap = c > 0

        def fresh_rows(start):
            a, b = (ref[start : start + TOKENS, :] for ref in kv_refs)
            rows = [jnp.where(swap, b, a), jnp.where(swap, a, b)]
            return jnp.concatenate(rows + [jnp.zeros((PAGE - BLOCK, HEAD), BF)], axis=0)

        store(0, fresh_rows(row), fresh_rows(row + TOKENS))
        store(1, zero, zero)
        carry = (jnp.int32(0), jnp.int32(0))
    for s, ref in enumerate(kv_refs):
        oy, oc = (y + far_side) % NY, (c + s) % NC
        base = ((oy * NZ + z) * NC + oc) * PAGES

        def visit(i, carry, ref=ref, base=base):
            count, edge = carry
            page = ints[base + i]
            request = (page >= PAGES_REQ).astype(jnp.int32)
            live = prefix - (page - request * PAGES_REQ) * PAGE
            mine = request == y
            whole = mine & (live >= PAGE)
            some = mine & (live > 0) & (live < PAGE)

            @pl.when(whole | some)
            def _():
                store(jnp.where(whole, count + 2, 1), ref[span(i), :], ref[span(PAGES + i), :])

            return count + whole.astype(jnp.int32), jnp.where(some, live, edge)

        carry = lax.fori_loop(0, PAGES, visit, carry)
    full, edge = carry
    largest = [ref[KV_ROWS:, :].astype(F32) for ref in kv_refs]
    if far_side:
        largest.append(square_in[...])
        for k in range(TILE - 1):
            store(full + 2 + k, zero, zero)
    info[0] = full
    info[1] = edge
    info[2] = ints[NY * PAGES_REQ + NY + y]
    square[...] = functools.reduce(jnp.maximum, largest)


def sort_pages(far_side, ints, kv, before=()):
    slots = SLOTS if far_side else NEAR_SLOTS
    pages = jax.ShapeDtypeStruct((slots * PAGE, HEAD), BF)
    operands = []
    if before:
        keys, values, info, square = before
        operands = [info, keys, values, square]
    return pl.pallas_call(
        functools.partial(sort_kernel, far_side),
        out_shape=[pages, pages, jax.ShapeDtypeStruct((4,), jnp.int32), jax.ShapeDtypeStruct((TOKENS, HEAD), F32)],
        in_specs=([SMEM] * 2 + [VMEM] * 3 if before else [SMEM]) + [VMEM] * 2,
        out_specs=[VMEM, VMEM, SMEM, VMEM],
        compiler_params=pltpu.CompilerParams(vmem_limit_bytes=12 * 2**20),
        cost_estimate=pl.CostEstimate(flops=0, bytes_accessed=2**20, transcendentals=0),
        name="sort_pages",
    )(ints, *operands, *kv)


def gather_kernel(*refs):
    q_refs, (q_all, square) = refs[:NZ], refs[NZ:]
    for h in range(HEADS):
        for k in range(NZ):
            at = slice(h * ROWS + k * BLOCK, h * ROWS + (k + 1) * BLOCK)
            q_all[at, :] = q_refs[k][:, h * HEAD : (h + 1) * HEAD]
    square[0] = jnp.max(largest_square(q_all[...])) * (SCALE * SCALE)


def gather_rows(q_blocks):
    return pl.pallas_call(
        gather_kernel,
        out_shape=[jax.ShapeDtypeStruct((HEADS * ROWS, HEAD), BF), jax.ShapeDtypeStruct((1,), F32)],
        in_specs=[VMEM] * NZ,
        out_specs=[VMEM, SMEM],
        compiler_params=pltpu.CompilerParams(vmem_limit_bytes=8 * 2**20),
        cost_estimate=pl.CostEstimate(flops=0, bytes_accessed=2**20, transcendentals=0),
        name="gather_rows",
    )(*q_blocks)


def attend_kernel(info, q_square, q_all, keys, values, square, *refs):
    out_refs, (acc, peak) = refs[:NZ], refs[NZ:]
    _, z, _ = place(lax.axis_index("ctx"))
    full, edge, fresh = info[0], info[1], info[2]
    total = full + 2
    acc[...] = jnp.zeros(acc.shape, F32)
    small = q_square[0] * jnp.max(square[...]) <= SAFE * SAFE
    peak[...] = jnp.full(peak.shape, jnp.where(small, 0.0, FLOOR), F32)
    lane = lax.broadcasted_iota(jnp.int32, (ROWS, PAGE), 1)
    offset = jnp.concatenate(
        [
            lax.rem(z - d + NZ, NZ) * BLOCK + lax.broadcasted_iota(jnp.int32, (BLOCK, PAGE), 0)
            for d in OFFSETS
        ],
        axis=0,
    )
    key_offset = z * BLOCK + lane
    new_limit = jnp.where((lane < BLOCK) & (key_offset < fresh), key_offset, 2 * ROWS)
    new_ok = (new_limit <= offset).astype(jnp.int32)
    ones = jnp.ones((KEYS, HEAD), BF)

    def visit_tile(masked, shifted, t, _):
        at = pl.ds(pl.multiple_of(t * KEYS, KEYS), KEYS)
        kt = keys[at, :]
        vt = jnp.concatenate([values[at, :], ones], axis=1)
        allowed = []
        if masked:
            for k in range(TILE):
                slot = t * TILE + k
                limit = jnp.where(slot == 1, edge, jnp.where(slot < total, PAGE, 0))
                cached = (lane < limit).astype(jnp.int32)
                allowed.append(jnp.concatenate([jnp.where(slot == 0, new_ok, cached)] * STACK, axis=0) > 0)
        for g in range(0, HEADS * ROWS, STACK * ROWS):
            at = slice(g, g + STACK * ROWS)
            s = lax.dot_general(q_all[at, :], kt, (((1,), (1,)), ((), ())), preferred_element_type=F32)
            parts = [s[:, k * PAGE : (k + 1) * PAGE] for k in range(TILE)]
            if masked:
                parts = [jnp.where(a, p, MASKED) for a, p in zip(allowed, parts)]
            if shifted:
                top = functools.reduce(jnp.maximum, parts)
                old = peak[at, :]
                new = jnp.maximum(old, jnp.max(top, axis=1, keepdims=True))
                shift = new * SCALE
                w = jnp.concatenate([jnp.exp2(p * SCALE - shift).astype(BF) for p in parts], axis=1)
                alpha = jnp.exp2((old - new) * SCALE)
                more = jnp.dot(w, vt, preferred_element_type=F32)
                acc[at, :] = acc[at, :] * jnp.concatenate([alpha, alpha], axis=1) + more
                peak[at, :] = new
            else:
                w = jnp.concatenate([jnp.exp2(p * SCALE).astype(BF) for p in parts], axis=1)
                acc[at, :] = acc[at, :] + jnp.dot(w, vt, preferred_element_type=F32)
        return 0

    whole_tiles = total // TILE
    tiles = (total + TILE - 1) // TILE

    def visit_all(shifted):
        last = jnp.maximum(whole_tiles, 1)
        lax.fori_loop(0, 1, functools.partial(visit_tile, True, shifted), 0)
        lax.fori_loop(1, last, functools.partial(visit_tile, False, shifted), 0)
        lax.fori_loop(last, tiles, functools.partial(visit_tile, True, shifted), 0)

    pl.when(small)(functools.partial(visit_all, False))
    pl.when(jnp.logical_not(small))(functools.partial(visit_all, True))

    logs = jnp.zeros((ROWS, PAGE), F32)
    for h in range(HEADS):
        at = slice(h * ROWS, (h + 1) * ROWS)
        weight = acc[at, HEAD:]
        kept = jnp.where(weight > 0, weight, 1.0)
        out = (acc[at, :HEAD] / kept).astype(BF)
        log_total = jnp.where(weight > 0, peak[at, :] * SCALE + jnp.log(kept) * math.log2(math.e), MASKED)
        high = log_total.astype(BF).astype(F32)
        rest = log_total - high
        mid = rest.astype(BF).astype(F32)
        for place_at, part in enumerate((high, mid, rest - mid)):
            logs = jnp.where(lane == place_at * HEADS + h, part, logs)
        for k in range(NZ):
            out_refs[k][:, h * HEAD : (h + 1) * HEAD] = out[k * BLOCK : (k + 1) * BLOCK, :]
    logs = logs.astype(BF)
    for k in range(NZ):
        out_refs[k][:, HALF:] = logs[k * BLOCK : (k + 1) * BLOCK, :]


def attend(info, q_square, q_all, keys, values, square):
    total = HEADS * ROWS
    return pl.pallas_call(
        attend_kernel,
        out_shape=[jax.ShapeDtypeStruct((BLOCK, WIDE), BF)] * NZ,
        in_specs=[SMEM] * 2 + [VMEM] * 4,
        out_specs=[VMEM] * NZ,
        scratch_shapes=[pltpu.VMEM((total, 2 * HEAD), F32), pltpu.VMEM((total, PAGE), F32)],
        compiler_params=pltpu.CompilerParams(vmem_limit_bytes=16 * 2**20),
        cost_estimate=pl.CostEstimate(
            flops=4 * total * 24 * PAGE * HEAD, bytes_accessed=4 * 2**20, transcendentals=total * 24 * PAGE
        ),
        name="attend",
    )(info, q_square, q_all, keys, values, square)


def weigh(blocks):
    logs = []
    for ref in blocks:
        part = ref[:, HALF:].astype(F32)
        logs.append(part + pltpu.roll(part, PAGE - HEADS, 1) + pltpu.roll(part, PAGE - 2 * HEADS, 1))
    top = functools.reduce(jnp.maximum, logs)
    weights = [jnp.exp2(g - top) for g in logs]
    return top, weights, functools.reduce(jnp.add, weights)


def blend(blocks, weights, out):
    for h in range(HEADS):
        at = slice(h * HEAD, (h + 1) * HEAD)
        terms = [ref[:, at].astype(F32) * w[:, h : h + 1] for ref, w in zip(blocks, weights)]
        out[:, at] = functools.reduce(jnp.add, terms).astype(BF)


def relay_kernel(a0, a1, a2, b0, b1, out_a, out_b):
    lane = lax.broadcasted_iota(jnp.int32, (BLOCK, PAGE), 1)
    for blocks, out in (((a0, a1, a2), out_a), ((b0, b1), out_b)):
        top, weights, total = weigh(blocks)
        scale = 1.0 / total
        blend(blocks, [w * scale for w in weights], out)
        log_total = jnp.where(lane < HEADS, top + jnp.log(total) * math.log2(math.e), 0.0)
        high = log_total.astype(BF).astype(F32)
        rest = log_total - high
        mid = rest.astype(BF).astype(F32)
        packed = high + pltpu.roll(mid, HEADS, 1) + pltpu.roll(rest - mid, 2 * HEADS, 1)
        out[:, HALF:] = packed.astype(BF)


def relay(blocks):
    return pl.pallas_call(
        relay_kernel,
        out_shape=[jax.ShapeDtypeStruct((BLOCK, WIDE), BF)] * 2,
        in_specs=[VMEM] * 5,
        out_specs=[VMEM] * 2,
        compiler_params=pltpu.CompilerParams(vmem_limit_bytes=4 * 2**20),
        cost_estimate=pl.CostEstimate(flops=2**20, bytes_accessed=2**20, transcendentals=0),
        name="relay",
    )(*blocks)


def merge_kernel(new_count, *refs):
    blocks, out = refs[:-1], refs[-1]
    y, z, _ = place(lax.axis_index("ctx"))
    _, weights, total = weigh(blocks)
    offset = z * BLOCK + lax.broadcasted_iota(jnp.int32, (BLOCK, PAGE), 0)
    scale = jnp.where(offset < new_count[y], 1.0 / total, 0.0)
    blend(blocks, [w * scale for w in weights], out)


def merge(new_count, blocks):
    return pl.pallas_call(
        merge_kernel,
        out_shape=jax.ShapeDtypeStruct((BLOCK, HALF), BF),
        in_specs=[SMEM] + [VMEM] * len(blocks),
        out_specs=VMEM,
        compiler_params=pltpu.CompilerParams(vmem_limit_bytes=4 * 2**20),
        cost_estimate=pl.CostEstimate(flops=2**20, bytes_accessed=2**20, transcendentals=0),
        name="merge",
    )(new_count, *blocks)


def project_kernel(*refs):
    pieces, weight, out, rows = refs[:8], refs[8], refs[9], refs[10]
    y, z, c = place(lax.axis_index("ctx"))
    for s in range(4):
        request, half = (y + s // 2) % NY, (c + s % 2) % NC
        columns = pl.ds(pl.multiple_of(half * HALF, HALF), HALF)
        for k, d in enumerate(OFFSETS):
            ref, first = (pieces[2 * s], 0) if k < 5 else (pieces[2 * s + 1], 5)
            at = pl.multiple_of(request * ROWS + lax.rem(z - d + NZ, NZ) * BLOCK, BLOCK)
            rows[pl.ds(at, BLOCK), columns] = ref[(k - first) * BLOCK : (k - first + 1) * BLOCK, :]
    for r in range(0, NY * ROWS, 256):
        out[r : r + 256, :] = jnp.dot(rows[r : r + 256, :], weight[...], preferred_element_type=F32).astype(BF)


def project(pieces, weight):
    tokens, depth, columns = NY * ROWS, NC * HALF, weight.shape[1]
    return pl.pallas_call(
        project_kernel,
        out_shape=jax.ShapeDtypeStruct((tokens, columns), BF),
        in_specs=[VMEM] * 9,
        out_specs=VMEM,
        scratch_shapes=[pltpu.VMEM((tokens, depth), BF)],
        compiler_params=pltpu.CompilerParams(vmem_limit_bytes=12 * 2**20),
        cost_estimate=pl.CostEstimate(flops=2 * tokens * depth * columns, bytes_accessed=5 * 2**20, transcendentals=0),
        name="project",
    )(*pieces, weight)


def local(
    queries,
    rotated_new_keys,
    fresh_token_values,
    paged_key_cache,
    paged_value_cache,
    out_weight,
    prefix_len,
    new_count,
    page_map,
):
    c = lax.axis_index("ctx") % NC
    slots = PAGES * PAGE
    left, right = queries[:, :HALF], queries[:, HALF:]
    keep, send = jnp.where(c == 0, left, right), jnp.where(c == 0, right, left)
    send, new_keys = lax.optimization_barrier((send, rotated_new_keys))
    got = moved(send, dc=1)
    kv_own = pack(
        paged_key_cache.reshape(slots, HEAD), paged_value_cache.reshape(slots, HEAD), new_keys, fresh_token_values
    )
    kv_own, got = lax.optimization_barrier((kv_own, got))
    kv_other = moved(kv_own, dy=1)
    block = jnp.where(c == 0, jnp.concatenate([keep, got]), jnp.concatenate([got, keep]))
    q_near = near(block)
    q_far, _ = far(q_near)
    ints = jnp.concatenate([page_map, prefix_len, new_count])
    kv_mine, q_near = lax.optimization_barrier(([kv_own, moved(kv_own, dc=1), ints], q_near))
    *kv_mine, ints = kv_mine
    sorted_near = sort_pages(0, ints, kv_mine)
    kv_other, q_far, sorted_near = lax.optimization_barrier((kv_other, q_far, sorted_near))
    kv_far = [kv_other, moved(kv_other, dc=1)]
    q_all, q_square = gather_rows([block] + q_near + q_far)
    kv_far, q_all = lax.optimization_barrier((kv_far, q_all))
    keys, values, info, square = sort_pages(1, ints, kv_far, sorted_near)
    parts = attend(info, q_square, q_all, keys, values, square)
    far_two, far_one, far_other = moved(parts[7], dz=-2), moved(parts[5], dz=-1), moved(parts[6], dz=1)
    side = [moved(parts[1], dz=-1), moved(parts[2], dz=1)]
    behind, ahead = relay([parts[3], far_one, far_two, parts[4], far_other])
    back = [parts[0]] + side + [moved(behind, dz=-2), moved(ahead, dz=2)]
    attn = merge(new_count, back)
    a_near = near(attn)
    a_far, _ = far(a_near)
    first, second = jnp.concatenate([attn] + a_near), jnp.concatenate(a_far)
    pieces = []
    for one, two in ((first, second), (moved(first, dy=1), moved(second, dy=1))):
        pieces += [one, two, moved(one, dc=1), moved(two, dc=1)]
    terms = project(pieces, out_weight)
    tp = lax.axis_size("tp")
    terms = terms.reshape(tp, terms.shape[0] // tp, terms.shape[1])
    swapped = lax.all_to_all(terms, "tp", split_axis=0, concat_axis=0, tiled=True)
    return jnp.sum(swapped.astype(F32), axis=0).astype(BF)


def solution(mesh):
    placed = (
        P("ctx", "tp"),
        P("ctx", "tp"),
        P("ctx", "tp"),
        P("ctx", None, "tp"),
        P("ctx", None, "tp"),
        P("tp", "ctx"),
        P(),
        P(),
        P(),
    )
    return jax.shard_map(local, mesh=mesh, in_specs=placed, out_specs=P("tp", "ctx"), check_vma=False)
```

```python
import functools
import math

import jax
import jax.numpy as jnp
from jax import lax
from jax.experimental import pallas as pl
from jax.experimental.pallas import tpu as pltpu
from jax.sharding import PartitionSpec as P

NY, NZ, NC = 2, 8, 2
HEAD = 128
GROUP = 16
HEADS = GROUP // NC
PAGE = 128
PAGES = 12
TOKENS = 16
BLOCK = TOKENS * NC
ROWS = BLOCK * NZ
PAGES_REQ = 192
HALF = HEADS * HEAD
WIDE = HALF + 128
TILE = 4
STACK = 1
KEYS = TILE * PAGE
SLOTS = 56
NEAR_SLOTS = 26
KV_ROWS = 2 * PAGES * PAGE + 2 * TOKENS
MASKED = -1e30
FLOOR = -1e29
SAFE = 100.0
SCALE = HEAD**-0.5 * math.log2(math.e)
OFFSETS = (0, 1, -1, 2, -2, 3, -3, 4)
BF = jnp.bfloat16
F32 = jnp.float32
VMEM = pl.BlockSpec(memory_space=pltpu.VMEM)
SMEM = pl.BlockSpec(memory_space=pltpu.SMEM)


def place(i):
    return i // (NZ * NC), (i // NC) % NZ, i % NC


def moved(x, dy=0, dz=0, dc=0):
    pairs = []
    for i in range(NY * NZ * NC):
        y, z, c = place(i)
        pairs.append((i, (((y + dy) % NY) * NZ + (z + dz) % NZ) * NC + (c + dc) % NC))
    return lax.ppermute(x, "ctx", pairs)


def near(block):
    return [moved(block, dz=d) for d in OFFSETS[1:5]]


def far(got, first=()):
    got, first = lax.optimization_barrier((got, first))
    return [moved(got[2], dz=1), moved(got[3], dz=-1), moved(got[2], dz=2)], first


def largest_square(rows):
    x = rows.astype(F32)
    sums = jnp.dot((x * x).astype(BF), jnp.ones((HEAD, HEAD), BF), preferred_element_type=F32)
    return jnp.max(sums, axis=0, keepdims=True) * 1.01


def pack_kernel(k, v, new_k, new_v, out, sems):
    slots = PAGES * PAGE
    half = slots // 2
    pieces = [(k, i * half, i * half, half) for i in range(2)]
    pieces += [(v, i * half, slots + i * half, half) for i in range(2)]
    pieces += [(new_k, 0, 2 * slots, TOKENS), (new_v, 0, 2 * slots + TOKENS, TOKENS)]
    copies = [
        pltpu.make_async_copy(ref.at[pl.ds(start, n)], out.at[pl.ds(to, n)], sems.at[i])
        for i, (ref, start, to, n) in enumerate(pieces)
    ]
    for copy in copies:
        copy.start()
    for copy in copies:
        copy.wait()
    square = jnp.maximum(largest_square(out[:slots, :]), largest_square(out[2 * slots : 2 * slots + TOKENS, :]))
    out[KV_ROWS:, :] = jnp.broadcast_to(square * 1.01, (TOKENS, HEAD)).astype(BF)


def pack(k, v, new_k, new_v):
    return pl.pallas_call(
        pack_kernel,
        out_shape=jax.ShapeDtypeStruct((KV_ROWS + TOKENS, HEAD), BF),
        in_specs=[pl.BlockSpec(memory_space=pltpu.HBM)] * 4,
        out_specs=VMEM,
        scratch_shapes=[pltpu.SemaphoreType.DMA((6,))],
        compiler_params=pltpu.CompilerParams(vmem_limit_bytes=60 * 2**20),
        cost_estimate=pl.CostEstimate(flops=0, bytes_accessed=2 * KV_ROWS * HEAD * 2, transcendentals=0),
        name="pack",
    )(k, v, new_k, new_v)


def sort_kernel(far_side, ints, *refs):
    if far_side:
        before, keys_in, values_in, square_in = refs[:4]
        refs = refs[4:]
    kv_refs, (keys, values, info, square) = refs[:2], refs[2:]
    y, z, c = place(lax.axis_index("ctx"))
    prefix = ints[NY * PAGES_REQ + y]

    def span(slot):
        return pl.ds(pl.multiple_of(slot * PAGE, PAGE), PAGE)

    def store(slot, key, value):
        keys[span(slot), :] = key
        values[span(slot), :] = value

    zero = jnp.zeros((PAGE, HEAD), BF)
    if far_side:
        held = slice(0, NEAR_SLOTS * PAGE)
        keys[held, :] = keys_in[held, :]
        values[held, :] = values_in[held, :]
        carry = (before[0], before[1])
    else:
        row = 2 * PAGES * PAGE
        swap = c > 0

        def fresh_rows(start):
            a, b = (ref[start : start + TOKENS, :] for ref in kv_refs)
            rows = [jnp.where(swap, b, a), jnp.where(swap, a, b)]
            return jnp.concatenate(rows + [jnp.zeros((PAGE - BLOCK, HEAD), BF)], axis=0)

        store(0, fresh_rows(row), fresh_rows(row + TOKENS))
        store(1, zero, zero)
        carry = (jnp.int32(0), jnp.int32(0))
    for s, ref in enumerate(kv_refs):
        oy, oc = (y + far_side) % NY, (c + s) % NC
        base = ((oy * NZ + z) * NC + oc) * PAGES

        def visit(i, carry, ref=ref, base=base):
            count, edge = carry
            page = ints[base + i]
            request = (page >= PAGES_REQ).astype(jnp.int32)
            live = prefix - (page - request * PAGES_REQ) * PAGE
            mine = request == y
            whole = mine & (live >= PAGE)
            some = mine & (live > 0) & (live < PAGE)

            @pl.when(whole | some)
            def _():
                store(jnp.where(whole, count + 2, 1), ref[span(i), :], ref[span(PAGES + i), :])

            return count + whole.astype(jnp.int32), jnp.where(some, live, edge)

        carry = lax.fori_loop(0, PAGES, visit, carry)
    full, edge = carry
    largest = [ref[KV_ROWS:, :].astype(F32) for ref in kv_refs]
    if far_side:
        largest.append(square_in[...])
        for k in range(TILE - 1):
            store(full + 2 + k, zero, zero)
    info[0] = full
    info[1] = edge
    info[2] = ints[NY * PAGES_REQ + NY + y]
    square[...] = functools.reduce(jnp.maximum, largest)


def sort_pages(far_side, ints, kv, before=()):
    slots = SLOTS if far_side else NEAR_SLOTS
    pages = jax.ShapeDtypeStruct((slots * PAGE, HEAD), BF)
    operands = []
    if before:
        keys, values, info, square = before
        operands = [info, keys, values, square]
    return pl.pallas_call(
        functools.partial(sort_kernel, far_side),
        out_shape=[pages, pages, jax.ShapeDtypeStruct((4,), jnp.int32), jax.ShapeDtypeStruct((TOKENS, HEAD), F32)],
        in_specs=([SMEM] * 2 + [VMEM] * 3 if before else [SMEM]) + [VMEM] * 2,
        out_specs=[VMEM, VMEM, SMEM, VMEM],
        compiler_params=pltpu.CompilerParams(vmem_limit_bytes=12 * 2**20),
        cost_estimate=pl.CostEstimate(flops=0, bytes_accessed=2**20, transcendentals=0),
        name="sort_pages",
    )(ints, *operands, *kv)


def gather_kernel(*refs):
    q_refs, (q_all, square) = refs[:NZ], refs[NZ:]
    for h in range(HEADS):
        for k in range(NZ):
            at = slice(h * ROWS + k * BLOCK, h * ROWS + (k + 1) * BLOCK)
            q_all[at, :] = q_refs[k][:, h * HEAD : (h + 1) * HEAD]
    square[0] = jnp.max(largest_square(q_all[...])) * (SCALE * SCALE)


def gather_rows(q_blocks):
    return pl.pallas_call(
        gather_kernel,
        out_shape=[jax.ShapeDtypeStruct((HEADS * ROWS, HEAD), BF), jax.ShapeDtypeStruct((1,), F32)],
        in_specs=[VMEM] * NZ,
        out_specs=[VMEM, SMEM],
        compiler_params=pltpu.CompilerParams(vmem_limit_bytes=8 * 2**20),
        cost_estimate=pl.CostEstimate(flops=0, bytes_accessed=2**20, transcendentals=0),
        name="gather_rows",
    )(*q_blocks)


def attend_kernel(info, q_square, q_all, keys, values, square, *refs):
    out_refs, (acc, peak) = refs[:NZ], refs[NZ:]
    _, z, _ = place(lax.axis_index("ctx"))
    full, edge, fresh = info[0], info[1], info[2]
    total = full + 2
    acc[...] = jnp.zeros(acc.shape, F32)
    small = q_square[0] * jnp.max(square[...]) <= SAFE * SAFE
    peak[...] = jnp.full(peak.shape, jnp.where(small, 0.0, FLOOR), F32)
    lane = lax.broadcasted_iota(jnp.int32, (ROWS, PAGE), 1)
    offset = jnp.concatenate(
        [
            lax.rem(z - d + NZ, NZ) * BLOCK + lax.broadcasted_iota(jnp.int32, (BLOCK, PAGE), 0)
            for d in OFFSETS
        ],
        axis=0,
    )
    key_offset = z * BLOCK + lane
    new_limit = jnp.where((lane < BLOCK) & (key_offset < fresh), key_offset, 2 * ROWS)
    new_ok = (new_limit <= offset).astype(jnp.int32)
    ones = jnp.ones((KEYS, HEAD), BF)

    def visit_tile(masked, shifted, t, _):
        at = pl.ds(pl.multiple_of(t * KEYS, KEYS), KEYS)
        kt = keys[at, :]
        vt = jnp.concatenate([values[at, :], ones], axis=1)
        allowed = []
        if masked:
            for k in range(TILE):
                slot = t * TILE + k
                limit = jnp.where(slot == 1, edge, jnp.where(slot < total, PAGE, 0))
                cached = (lane < limit).astype(jnp.int32)
                allowed.append(jnp.concatenate([jnp.where(slot == 0, new_ok, cached)] * STACK, axis=0) > 0)
        for g in range(0, HEADS * ROWS, STACK * ROWS):
            at = slice(g, g + STACK * ROWS)
            s = lax.dot_general(q_all[at, :], kt, (((1,), (1,)), ((), ())), preferred_element_type=F32)
            parts = [s[:, k * PAGE : (k + 1) * PAGE] for k in range(TILE)]
            if masked:
                parts = [jnp.where(a, p, MASKED) for a, p in zip(allowed, parts)]
            if shifted:
                top = functools.reduce(jnp.maximum, parts)
                old = peak[at, :]
                new = jnp.maximum(old, jnp.max(top, axis=1, keepdims=True))
                shift = new * SCALE
                w = jnp.concatenate([jnp.exp2(p * SCALE - shift).astype(BF) for p in parts], axis=1)
                alpha = jnp.exp2((old - new) * SCALE)
                more = jnp.dot(w, vt, preferred_element_type=F32)
                acc[at, :] = acc[at, :] * jnp.concatenate([alpha, alpha], axis=1) + more
                peak[at, :] = new
            else:
                w = jnp.concatenate([jnp.exp2(p * SCALE).astype(BF) for p in parts], axis=1)
                acc[at, :] = acc[at, :] + jnp.dot(w, vt, preferred_element_type=F32)
        return 0

    whole_tiles = total // TILE
    tiles = (total + TILE - 1) // TILE

    def visit_all(shifted):
        last = jnp.maximum(whole_tiles, 1)
        lax.fori_loop(0, 1, functools.partial(visit_tile, True, shifted), 0)
        lax.fori_loop(1, last, functools.partial(visit_tile, False, shifted), 0)
        lax.fori_loop(last, tiles, functools.partial(visit_tile, True, shifted), 0)

    pl.when(small)(functools.partial(visit_all, False))
    pl.when(jnp.logical_not(small))(functools.partial(visit_all, True))

    logs = jnp.zeros((ROWS, PAGE), F32)
    for h in range(HEADS):
        at = slice(h * ROWS, (h + 1) * ROWS)
        weight = acc[at, HEAD:]
        kept = jnp.where(weight > 0, weight, 1.0)
        out = (acc[at, :HEAD] / kept).astype(BF)
        log_total = jnp.where(weight > 0, peak[at, :] * SCALE + jnp.log(kept) * math.log2(math.e), MASKED)
        high = log_total.astype(BF).astype(F32)
        rest = log_total - high
        mid = rest.astype(BF).astype(F32)
        for place_at, part in enumerate((high, mid, rest - mid)):
            logs = jnp.where(lane == place_at * HEADS + h, part, logs)
        for k in range(NZ):
            out_refs[k][:, h * HEAD : (h + 1) * HEAD] = out[k * BLOCK : (k + 1) * BLOCK, :]
    logs = logs.astype(BF)
    for k in range(NZ):
        out_refs[k][:, HALF:] = logs[k * BLOCK : (k + 1) * BLOCK, :]


def attend(info, q_square, q_all, keys, values, square):
    total = HEADS * ROWS
    return pl.pallas_call(
        attend_kernel,
        out_shape=[jax.ShapeDtypeStruct((BLOCK, WIDE), BF)] * NZ,
        in_specs=[SMEM] * 2 + [VMEM] * 4,
        out_specs=[VMEM] * NZ,
        scratch_shapes=[pltpu.VMEM((total, 2 * HEAD), F32), pltpu.VMEM((total, PAGE), F32)],
        compiler_params=pltpu.CompilerParams(vmem_limit_bytes=16 * 2**20),
        cost_estimate=pl.CostEstimate(
            flops=4 * total * 24 * PAGE * HEAD, bytes_accessed=4 * 2**20, transcendentals=total * 24 * PAGE
        ),
        name="attend",
    )(info, q_square, q_all, keys, values, square)


def weigh(blocks):
    logs = []
    for ref in blocks:
        part = ref[:, HALF:].astype(F32)
        logs.append(part + pltpu.roll(part, PAGE - HEADS, 1) + pltpu.roll(part, PAGE - 2 * HEADS, 1))
    top = functools.reduce(jnp.maximum, logs)
    weights = [jnp.exp2(g - top) for g in logs]
    return top, weights, functools.reduce(jnp.add, weights)


def blend(blocks, weights, out):
    for h in range(HEADS):
        at = slice(h * HEAD, (h + 1) * HEAD)
        terms = [ref[:, at].astype(F32) * w[:, h : h + 1] for ref, w in zip(blocks, weights)]
        out[:, at] = functools.reduce(jnp.add, terms).astype(BF)


def relay_kernel(*refs):
    blocks, out = refs[:-1], refs[-1]
    lane = lax.broadcasted_iota(jnp.int32, (BLOCK, PAGE), 1)
    top, weights, total = weigh(blocks)
    scale = 1.0 / total
    blend(blocks, [w * scale for w in weights], out)
    log_total = jnp.where(lane < HEADS, top + jnp.log(total) * math.log2(math.e), 0.0)
    high = log_total.astype(BF).astype(F32)
    rest = log_total - high
    mid = rest.astype(BF).astype(F32)
    packed = high + pltpu.roll(mid, HEADS, 1) + pltpu.roll(rest - mid, 2 * HEADS, 1)
    out[:, HALF:] = packed.astype(BF)


def relay(blocks):
    return pl.pallas_call(
        relay_kernel,
        out_shape=jax.ShapeDtypeStruct((BLOCK, WIDE), BF),
        in_specs=[VMEM] * len(blocks),
        out_specs=VMEM,
        compiler_params=pltpu.CompilerParams(vmem_limit_bytes=4 * 2**20),
        cost_estimate=pl.CostEstimate(flops=2**20, bytes_accessed=2**20, transcendentals=0),
        name="relay",
    )(*blocks)


def merge_kernel(new_count, *refs):
    blocks, out = refs[:-1], refs[-1]
    y, z, _ = place(lax.axis_index("ctx"))
    _, weights, total = weigh(blocks)
    offset = z * BLOCK + lax.broadcasted_iota(jnp.int32, (BLOCK, PAGE), 0)
    scale = jnp.where(offset < new_count[y], 1.0 / total, 0.0)
    blend(blocks, [w * scale for w in weights], out)


def merge(new_count, blocks):
    return pl.pallas_call(
        merge_kernel,
        out_shape=jax.ShapeDtypeStruct((BLOCK, HALF), BF),
        in_specs=[SMEM] + [VMEM] * len(blocks),
        out_specs=VMEM,
        compiler_params=pltpu.CompilerParams(vmem_limit_bytes=4 * 2**20),
        cost_estimate=pl.CostEstimate(flops=2**20, bytes_accessed=2**20, transcendentals=0),
        name="merge",
    )(new_count, *blocks)


def project_kernel(*refs):
    pieces, weight, out, rows = refs[:8], refs[8], refs[9], refs[10]
    y, z, c = place(lax.axis_index("ctx"))
    for s in range(4):
        request, half = (y + s // 2) % NY, (c + s % 2) % NC
        columns = pl.ds(pl.multiple_of(half * HALF, HALF), HALF)
        for k, d in enumerate(OFFSETS):
            ref, first = (pieces[2 * s], 0) if k < 5 else (pieces[2 * s + 1], 5)
            at = pl.multiple_of(request * ROWS + lax.rem(z - d + NZ, NZ) * BLOCK, BLOCK)
            rows[pl.ds(at, BLOCK), columns] = ref[(k - first) * BLOCK : (k - first + 1) * BLOCK, :]
    for r in range(0, NY * ROWS, 256):
        out[r : r + 256, :] = jnp.dot(rows[r : r + 256, :], weight[...], preferred_element_type=F32).astype(BF)


def project(pieces, weight):
    tokens, depth, columns = NY * ROWS, NC * HALF, weight.shape[1]
    return pl.pallas_call(
        project_kernel,
        out_shape=jax.ShapeDtypeStruct((tokens, columns), BF),
        in_specs=[VMEM] * 9,
        out_specs=VMEM,
        scratch_shapes=[pltpu.VMEM((tokens, depth), BF)],
        compiler_params=pltpu.CompilerParams(vmem_limit_bytes=12 * 2**20),
        cost_estimate=pl.CostEstimate(flops=2 * tokens * depth * columns, bytes_accessed=5 * 2**20, transcendentals=0),
        name="project",
    )(*pieces, weight)


def local(
    queries,
    rotated_new_keys,
    fresh_token_values,
    paged_key_cache,
    paged_value_cache,
    out_weight,
    prefix_len,
    new_count,
    page_map,
):
    c = lax.axis_index("ctx") % NC
    slots = PAGES * PAGE
    left, right = queries[:, :HALF], queries[:, HALF:]
    keep, send = jnp.where(c == 0, left, right), jnp.where(c == 0, right, left)
    send, new_keys = lax.optimization_barrier((send, rotated_new_keys))
    got = moved(send, dc=1)
    kv_own = pack(
        paged_key_cache.reshape(slots, HEAD), paged_value_cache.reshape(slots, HEAD), new_keys, fresh_token_values
    )
    kv_own, got = lax.optimization_barrier((kv_own, got))
    kv_other = moved(kv_own, dy=1)
    block = jnp.where(c == 0, jnp.concatenate([keep, got]), jnp.concatenate([got, keep]))
    q_near = near(block)
    q_far, _ = far(q_near)
    ints = jnp.concatenate([page_map, prefix_len, new_count])
    kv_mine, q_near = lax.optimization_barrier(([kv_own, moved(kv_own, dc=1), ints], q_near))
    *kv_mine, ints = kv_mine
    sorted_near = sort_pages(0, ints, kv_mine)
    kv_other, q_far, sorted_near = lax.optimization_barrier((kv_other, q_far, sorted_near))
    kv_far = [kv_other, moved(kv_other, dc=1)]
    q_all, q_square = gather_rows([block] + q_near + q_far)
    kv_far, q_all = lax.optimization_barrier((kv_far, q_all))
    keys, values, info, square = sort_pages(1, ints, kv_far, sorted_near)
    parts = attend(info, q_square, q_all, keys, values, square)
    ahead = moved(relay([parts[4], moved(parts[6], dz=1)]), dz=2)
    behind = moved(relay([parts[3], moved(parts[5], dz=-1), moved(parts[7], dz=-2)]), dz=-2)
    back = [parts[0], moved(parts[1], dz=-1), moved(parts[2], dz=1), behind, ahead]
    attn = merge(new_count, back)
    a_near = near(attn)
    a_far, _ = far(a_near)
    first, second = jnp.concatenate([attn] + a_near), jnp.concatenate(a_far)
    pieces = []
    for one, two in ((first, second), (moved(first, dy=1), moved(second, dy=1))):
        pieces += [one, two, moved(one, dc=1), moved(two, dc=1)]
    terms = project(pieces, out_weight)
    tp = lax.axis_size("tp")
    terms = terms.reshape(tp, terms.shape[0] // tp, terms.shape[1])
    swapped = lax.all_to_all(terms, "tp", split_axis=0, concat_axis=0, tiled=True)
    return jnp.sum(swapped.astype(F32), axis=0).astype(BF)


def solution(mesh):
    placed = (
        P("ctx", "tp"),
        P("ctx", "tp"),
        P("ctx", "tp"),
        P("ctx", None, "tp"),
        P("ctx", None, "tp"),
        P("tp", "ctx"),
        P(),
        P(),
        P(),
    )
    return jax.shard_map(local, mesh=mesh, in_specs=placed, out_specs=P("tp", "ctx"), check_vma=False)
```
